512 devices in a mesh: tile: 64 (over z, x, core), tm: 8 (over y).
Axes of the slice: x: 4, y: 8, z: 8, core: 2. Of those that a mesh axis runs over, the one named last changes fastest.
Arguments:
- video_slabs: bfloat16 [64, 32, 96, 4, 128], P('tile', 'tm'), may hold values from -6 to 6
- slab_links: int32 [64, 4], P('tile'), may hold values from -1 to 63, as said below
- slab_extents: int32 [64, 2], P('tile'), may hold values from 1 to 128, as said below
- norm1_gain: float32 [96], replicated, may hold values from 0.1 to 1.9
- conv1_weight: bfloat16 [96, 2592], replicated, may hold values from -0.125 to 0.125
- conv1_bias: float32 [96], replicated, may hold values from -3 to 3
- norm2_gain: float32 [96], replicated, may hold values from 0.1 to 1.9
- conv2_weight: bfloat16 [96, 2592], replicated, may hold values from -0.125 to 0.125
- conv2_bias: float32 [96], replicated, may hold values from -3 to 3
- down_weight: bfloat16 [96, 864], replicated, may hold values from -0.21875 to 0.21875
- down_bias: float32 [96], replicated, may hold values from -3 to 3
Outputs:
- encoded: bfloat16 [64, 32, 96, 128], P('tile', 'tm')
The draws below stay inside these ranges and needn't reach their ends.
Inputs may be any that keep to these rules, and one draw needn't show every extreme that they name: `slab_links`: row s holds the links of slab s on a canvas grid of 8 slabs a row, in the order up, down, left, right: s - 8, s + 8, s - 1 and s + 1, or -1 at the border of its clip. Linked slabs form whole rectangular clips: links are mutual, and the left link of the up link is the up link of the left link, likewise at every corner. `slab_extents`: row s holds the rows and the columns of slab s that lie inside its clip, counted from its top left corner; a slab with a down link has all 4 rows inside, one with a right link all 128 columns.
All inputs are finite; a program needn't handle non-finite values.
Results may differ from the reference program's by a relative error of at most 0.0052.
Values may be sent and summed in bfloat16 or wider, within the bound.
A program may use at most 64 MiB of HBM per device.

```python
import jax
import jax.numpy as jnp
from jax import lax

C = 96
SH = 4
SW = 128
GRID_COLUMN_COUNT = 8
SLABS = 64
FRAMES = 32


def layout(key):
    grid_rows = SLABS // GRID_COLUMN_COUNT
    key_rows, key_cols, key_high, key_wide = jax.random.split(key, 4)
    row_cut = jax.random.randint(key_rows, (grid_rows,), 0, 2, dtype=jnp.int32)
    row_cut = row_cut.at[0].set(0).at[grid_rows - 2].set(0).at[grid_rows - 1].set(1)
    col_cut = jax.random.randint(key_cols, (grid_rows, GRID_COLUMN_COUNT), 0, 2, dtype=jnp.int32)
    col_cut = col_cut.at[:, 0].set(0).at[:, GRID_COLUMN_COUNT - 1].set(1)
    row_index = jnp.arange(grid_rows, dtype=jnp.int32)
    col_index = jnp.arange(GRID_COLUMN_COUNT, dtype=jnp.int32)
    row_starts = jnp.concatenate([jnp.ones((1,), jnp.int32), row_cut[:-1]])
    band_start = lax.cummax(jnp.where(row_starts == 1, row_index, 0), axis=0)
    band_cuts = col_cut[band_start]
    col_starts = jnp.concatenate([jnp.ones((grid_rows, 1), jnp.int32), band_cuts[:, :-1]], axis=1)
    seg_start = lax.cummax(jnp.where(col_starts == 1, col_index[None, :], 0), axis=1)
    high_draw = jax.random.randint(key_high, (grid_rows, GRID_COLUMN_COUNT), 1, SH + 1, dtype=jnp.int32)
    wide_draw = jax.random.randint(key_wide, (grid_rows, GRID_COLUMN_COUNT), 1, SW + 1, dtype=jnp.int32)
    clip_rows = high_draw[band_start[:, None], seg_start]
    clip_cols = wide_draw[band_start[:, None], seg_start]
    shape_grid = (grid_rows, GRID_COLUMN_COUNT)
    down_ok = jnp.broadcast_to((row_cut == 0)[:, None], shape_grid)
    up_ok = jnp.broadcast_to(jnp.concatenate([jnp.zeros((1,), bool), row_cut[:-1] == 0])[:, None], shape_grid)
    right_ok = band_cuts == 0
    left_ok = jnp.concatenate([jnp.zeros((grid_rows, 1), bool), band_cuts[:, :-1] == 0], axis=1)
    slab_grid = jnp.arange(SLABS, dtype=jnp.int32).reshape(shape_grid)
    links_all = jnp.stack([jnp.where(up_ok, slab_grid - GRID_COLUMN_COUNT, -1), jnp.where(down_ok, slab_grid + GRID_COLUMN_COUNT, -1), jnp.where(left_ok, slab_grid - 1, -1), jnp.where(right_ok, slab_grid + 1, -1)], axis=-1).reshape(SLABS, 4)
    extents_all = jnp.stack([jnp.where(down_ok, SH, clip_rows), jnp.where(right_ok, SW, clip_cols)], axis=-1).reshape(SLABS, 2)
    return (links_all.astype(jnp.int32), extents_all.astype(jnp.int32))


def draw_slab_links(key, part):
    return layout(key)[0]


def draw_slab_extents(key, part):
    return layout(key)[1]


def block_scale(key, shape, cuts, least, top_value):
    loudness, own = 1.0, jax.random.fold_in(key, 6)
    for axis_at, blocks in cuts:
        heights = jnp.exp(jax.random.uniform(jax.random.fold_in(own, axis_at), (blocks,), jnp.float32, least / len(cuts), top_value / len(cuts)))
        loudness = loudness * jnp.repeat(heights, shape[axis_at] // blocks).reshape([-1 if axis == axis_at else 1 for axis in range(len(shape))])
    return loudness


def bell_draw(rng, dims, scale, most, cuts=(), kind=jnp.bfloat16):
    loudness = block_scale(rng, dims, cuts, -0.22, 0.18) if cuts else 1.0
    values = jax.random.normal(rng, dims, jnp.float32) * scale * loudness
    return jnp.minimum(jnp.maximum(values, -most), most).astype(kind)


def setup_inputs(seed: int = 0) -> dict:
    arg_keys = jax.random.split(jax.random.key(seed), 12)
    return {
        "video_slabs": bell_draw(arg_keys[0], (SLABS, FRAMES, C, SH, SW), 1.0, 6.0, ((0, 64), (1, 8))),
        "slab_links": draw_slab_links(jax.random.fold_in(arg_keys[11], 71), 0),
        "slab_extents": draw_slab_extents(jax.random.fold_in(arg_keys[11], 71), 0),
        "norm1_gain": jnp.clip(1.0 + 0.18 * jax.random.normal(arg_keys[3], (C,), jnp.float32), 0.1, 1.9),
        "conv1_weight": bell_draw(arg_keys[4], (C, 27 * C), (27 * C) ** -0.5, 0.125),
        "conv1_bias": bell_draw(arg_keys[5], (C,), 0.5, 3.0, (), jnp.float32),
        "norm2_gain": jnp.clip(1.0 + 0.18 * jax.random.normal(arg_keys[6], (C,), jnp.float32), 0.1, 1.9),
        "conv2_weight": bell_draw(arg_keys[7], (C, 27 * C), (27 * C) ** -0.5, 0.125),
        "conv2_bias": bell_draw(arg_keys[8], (C,), 0.5, 3.0, (), jnp.float32),
        "down_weight": bell_draw(arg_keys[9], (C, 9 * C), (9 * C) ** -0.5, 0.21875),
        "down_bias": bell_draw(arg_keys[10], (C,), 0.5, 3.0, (), jnp.float32),
    }


norm_eps = 1e-06

def activate(values, scale_gain, inside):
    widened = values.astype(jnp.float32)
    mean_square = lax.optimization_barrier(jnp.mean(widened * widened, axis=1, keepdims=True))
    normed = widened * lax.rsqrt(mean_square + norm_eps) * scale_gain[None, :, None, None]
    return (jax.nn.silu(normed) * inside).astype(jnp.bfloat16)

def inside_mask(slab_extents, slab_idx):
    row_ok = jnp.arange(SH, dtype=jnp.int32) < slab_extents[slab_idx, 0]
    col_ok = jnp.arange(SW, dtype=jnp.int32) < slab_extents[slab_idx, 1]
    return (row_ok[:, None] & col_ok[None, :]).astype(jnp.float32)

def output_mask(slab_extents, slab_links, slab_idx):
    half_rows = jnp.arange(SH // 2, dtype=jnp.int32)
    half_cols = jnp.arange(SW // 2, dtype=jnp.int32)
    row_ok = (2 * half_rows + 2 <= slab_extents[slab_idx, 0]) | (slab_links[slab_idx, 1] >= 0)
    col_ok = (2 * half_cols + 2 <= slab_extents[slab_idx, 1]) | (slab_links[slab_idx, 3] >= 0)
    return (row_ok[:, None] & col_ok[None, :]).astype(jnp.float32)

def tall_slab(field_all, slab_links, slab_idx):
    up_idx = slab_links[slab_idx, 0]
    down_idx = slab_links[slab_idx, 1]
    upper_row = field_all[jnp.maximum(up_idx, 0)][:, :, -1, :] * (up_idx >= 0).astype(field_all.dtype)
    lower_row = field_all[jnp.maximum(down_idx, 0)][:, :, 0, :] * (down_idx >= 0).astype(field_all.dtype)
    return jnp.concatenate([upper_row[:, :, None, :], field_all[slab_idx], lower_row[:, :, None, :]], axis=2)

def full_slab(field_all, slab_links, slab_idx):
    left_idx = slab_links[slab_idx, 2]
    right_idx = slab_links[slab_idx, 3]
    middle = tall_slab(field_all, slab_links, slab_idx)
    left_edge = tall_slab(field_all, slab_links, jnp.maximum(left_idx, 0))[:, :, :, -1:] * (left_idx >= 0).astype(field_all.dtype)
    right_edge = tall_slab(field_all, slab_links, jnp.maximum(right_idx, 0))[:, :, :, :1] * (right_idx >= 0).astype(field_all.dtype)
    return jnp.concatenate([left_edge, middle, right_edge], axis=3)

def lower_slab(field_all, slab_links, slab_idx):
    down_idx = slab_links[slab_idx, 1]
    lower_row = field_all[jnp.maximum(down_idx, 0)][:, :, 0, :] * (down_idx >= 0).astype(field_all.dtype)
    return jnp.concatenate([field_all[slab_idx], lower_row[:, :, None, :]], axis=2)

def lower_right(field_all, slab_links, slab_idx):
    right_idx = slab_links[slab_idx, 3]
    middle = lower_slab(field_all, slab_links, slab_idx)
    right_edge = lower_slab(field_all, slab_links, jnp.maximum(right_idx, 0))[:, :, :, :1] * (right_idx >= 0).astype(field_all.dtype)
    return jnp.concatenate([middle, right_edge], axis=3)

def causal_conv(padded, weight):
    channels = weight.shape[0]
    filter_weight = weight.reshape(channels, 3, 3, 3, channels)
    history = jnp.zeros((2,) + padded.shape[1:], padded.dtype)
    timed_input = jnp.concatenate([history, padded], axis=0)
    return lax.conv_general_dilated(timed_input[None], filter_weight, (1, 1, 1), 'VALID', dimension_numbers=('NDCHW', 'ODHWI', 'NDCHW'), preferred_element_type=jnp.float32)[0]

def down_conv(padded, weight):
    channels = weight.shape[0]
    filter_weight = weight.reshape(channels, 3, 3, channels)
    return lax.conv_general_dilated(padded, filter_weight, (2, 2), 'VALID', dimension_numbers=('NCHW', 'OHWI', 'NCHW'), preferred_element_type=jnp.float32)

def reference(video_slabs, slab_links, slab_extents, norm1_gain, conv1_weight, conv1_bias, norm2_gain, conv2_weight, conv2_bias, down_weight, down_bias):
    slab_ids = jnp.arange(video_slabs.shape[0], dtype=jnp.int32)

    def first_layer(slab_idx):
        return activate(video_slabs[slab_idx], norm1_gain, inside_mask(slab_extents, slab_idx))
    first_act = lax.map(first_layer, slab_ids)

    def second_layer(slab_idx):
        convolved_output = causal_conv(full_slab(first_act, slab_links, slab_idx), conv1_weight) + conv1_bias[None, :, None, None]
        return activate(convolved_output, norm2_gain, inside_mask(slab_extents, slab_idx))
    second_act = lax.map(second_layer, slab_ids)

    def third_layer(slab_idx):
        convolved_output = causal_conv(full_slab(second_act, slab_links, slab_idx), conv2_weight) + conv2_bias[None, :, None, None]
        summed = (video_slabs[slab_idx].astype(jnp.float32) + convolved_output) * inside_mask(slab_extents, slab_idx)
        return summed.astype(jnp.bfloat16)
    block_result = lax.map(third_layer, slab_ids)

    def fourth_layer(slab_idx):
        reduced = down_conv(lower_right(block_result, slab_links, slab_idx), down_weight) + down_bias[None, :, None, None]
        masked = reduced * output_mask(slab_extents, slab_links, slab_idx)
        return masked.astype(jnp.bfloat16).reshape(masked.shape[0], masked.shape[1], -1)
    return lax.map(fourth_layer, slab_ids)
```

```python
import functools

import jax
import jax.numpy as jnp
from jax import lax
from jax.experimental import pallas as pl
from jax.experimental.pallas import tpu as pltpu
from jax.sharding import PartitionSpec as P

GRID_COLUMN_COUNT = 8
MESH = pl.DeviceIdType.MESH
norm_eps = 1e-06
f32 = jnp.float32
bf16 = jnp.bfloat16

COPIES = 32


def kernel(
    grid_cols,
    grid_rows,
    groups,
    links,
    extents,
    x_hbm,
    g1_hbm,
    w1_hbm,
    b1_hbm,
    g2_hbm,
    w2_hbm,
    b2_hbm,
    wd_hbm,
    bd_hbm,
    out_hbm,
    x_raw,
    spread,
    x_rows,
    w_raw,
    wd_raw,
    vec_raw,
    vecs,
    w_conv,
    w_down,
    act1,
    act2,
    block,
    sums,
    edge_part,
    edge_sum,
    edge_out,
    edge_left,
    edge_right,
    result,
    load_sem,
    send_sem,
    recv_sem,
    store_sem,
):
    channels = vecs.shape[1]
    tile = lax.axis_index("tile")
    group = lax.axis_index("tm")
    grow, gcol = tile // grid_cols, tile % grid_cols
    up = (((grow + grid_rows - 1) % grid_rows) * grid_cols + gcol, group)
    down = (((grow + 1) % grid_rows) * grid_cols + gcol, group)
    left = (grow * grid_cols + (gcol + grid_cols - 1) % grid_cols, group)
    right = (grow * grid_cols + (gcol + 1) % grid_cols, group)
    later = (tile, (group + 1) % groups)
    before = (tile, (group + groups - 1) % groups)

    barrier = pltpu.get_barrier_semaphore()
    for device in (up, down, left, right, later, before):
        pl.semaphore_signal(barrier, inc=1, device_id=device, device_id_type=MESH)

    loads = []

    def load(src, dst):
        copy = pltpu.make_async_copy(src, dst, load_sem.at[len(loads)])
        copy.start()
        loads.append(copy)
        return copy

    x_loads = {t: load(x_hbm.at[t], x_raw.at[t]) for t in (2, 3, 0, 1)}
    vec_loads = [
        load(ref, vec_raw.at[i]) for i, ref in enumerate((g1_hbm, b1_hbm, g2_hbm, b2_hbm, bd_hbm))
    ]
    w1_load = load(w1_hbm, w_raw.at[0])
    w2_load = load(w2_hbm, w_raw.at[1])
    wd_load = load(wd_hbm, wd_raw)

    sends = []

    def send(src, dst, device):
        i = len(sends)
        copy = pltpu.make_async_remote_copy(
            src_ref=src,
            dst_ref=dst,
            send_sem=send_sem.at[i],
            recv_sem=recv_sem.at[i],
            device_id=device,
            device_id_type=MESH,
        )
        copy.start()
        sends.append(copy)
        return copy

    lane = lax.broadcasted_iota(jnp.int32, (channels, 128), 1)
    lane_row = lax.broadcasted_iota(jnp.int32, (1, 128), 1)
    up_ok, down_ok = links[0, 0] >= 0, links[0, 1] >= 0
    left_ok, right_ok = links[0, 2] >= 0, links[0, 3] >= 0
    row_count, col_count = extents[0, 0], extents[0, 1]

    def inside(r):
        cols = jnp.where(r < row_count, col_count, 0)
        return (lane_row < cols).astype(f32)

    def activate(values, gain, r):
        mean_square = jnp.mean(values * values, axis=0, keepdims=True)
        normed = values * lax.rsqrt(mean_square + norm_eps) * gain
        return (normed / (1.0 + jnp.exp(-normed)) * inside(r)).astype(bf16)

    for copy in vec_loads:
        copy.wait()
    diagonal = lax.broadcasted_iota(jnp.int32, (channels, channels), 0) == lax.broadcasted_iota(
        jnp.int32, (channels, channels), 1
    )
    for i in range(5):
        column = jnp.sum(jnp.where(diagonal, vec_raw[i], 0.0), axis=1, keepdims=True)
        vecs[i] = jnp.broadcast_to(column, (channels, 128))

    def first(t):
        x_loads[t].wait()
        spread[...] = x_raw[t].astype(f32)
        gain = vecs[0]
        for r in range(4):
            values = spread[pl.ds(r, channels, stride=4), :]
            x_rows[t, r] = values.astype(bf16)
            act1[2 + t, 1 + r] = activate(values, gain, r)

    def masked(ref, index, ok):
        ref[index] = jnp.where(ok, ref[index], jnp.zeros_like(ref[index]))

    def send_frames(act):
        return [
            send(act.at[4, pl.ds(1, 4)], act.at[0, pl.ds(1, 4)], later),
            send(act.at[5, pl.ds(1, 4)], act.at[1, pl.ds(1, 4)], later),
        ]

    def send_rows(act, f):
        frames = pl.ds(f, 2)
        return [
            send(act.at[frames, 4], act.at[frames, 0], down),
            send(act.at[frames, 1], act.at[frames, 5], up),
        ]

    def wait_rows(act, f, copies):
        copies[0].wait_recv()
        copies[1].wait_recv()
        for g in (f, f + 1):
            masked(act, (g, 0), up_ok)
            masked(act, (g, 5), down_ok)

    def edges(act, frames, rows, total):
        for f in frames:
            for r in rows:
                k = f * 6 + r
                moved = pltpu.roll(act[f, r].astype(f32), 2 * k + 1, 1)
                total = jnp.where(lane // 2 == k, moved, total)
        return total

    def send_edges(slot, total):
        edge_out[slot] = total.astype(bf16)
        return [
            send(edge_out.at[slot], edge_left.at[slot], right),
            send(edge_out.at[slot], edge_right.at[slot], left),
        ]

    def patches(act, t, r):
        return jnp.concatenate(
            [act[t + dt, r : r + 3].reshape(3 * channels, 128) for dt in range(3)], axis=0
        )

    def products(act, weight, t, rows):
        operand = jnp.concatenate([patches(act, t, r) for r in rows], axis=1)
        total = jnp.dot(weight[...], operand, preferred_element_type=f32)
        for i, r in enumerate(rows):
            sums[t, r] = total[:, 128 * i : 128 * i + 128]

    def received(slot):
        both = jnp.where(
            lane % 2 == 0,
            jnp.where(left_ok, edge_left[slot].astype(f32), 0.0),
            jnp.where(right_ok, edge_right[slot].astype(f32), 0.0),
        )
        return both

    def edge_products(cells, weight):
        operand = jnp.concatenate(
            [
                cells if dt + dr == 0 else pltpu.roll(cells, 128 - 2 * (6 * dt + dr), 1)
                for dt in range(3)
                for dr in range(3)
            ],
            axis=0,
        ).astype(bf16)
        west = jnp.dot(weight[:channels], operand, preferred_element_type=f32)
        east = jnp.dot(weight[2 * channels :], operand, preferred_element_type=f32)
        edge_sum[...] = jnp.where(
            lane % 2 == 1, pltpu.roll(west, 1, 1), pltpu.roll(east, 127, 1)
        )

    def convolved(t, r):
        k = 6 * t + r
        ends = pltpu.roll(edge_sum[...], 128 - (2 * k + 1), 1)
        west = jnp.where(lane == 0, ends, pltpu.roll(sums[t, r, :channels], 1, 1))
        east = jnp.where(lane == 127, ends, pltpu.roll(sums[t, r, 2 * channels :], 127, 1))
        return west + sums[t, r, channels : 2 * channels] + east

    def arrange(raw, taps, step, store):
        value = raw.astype(f32)
        for dc in range(3):
            parts = [
                value[:, (3 * tap + dc) * channels : (3 * tap + dc + 1) * channels]
                for tap in range(taps)
            ]
            store(dc, jnp.concatenate(parts, axis=1).astype(bf16))

    def store_conv(i):
        def put(dc, rows):
            w_conv[i, dc * channels : (dc + 1) * channels] = rows

        return put

    def store_down(dc, rows):
        w_down[dc * channels : (dc + 1) * channels] = rows

    zeros = jnp.zeros((channels, 128), f32)

    def conv_layer(layer, act, frame_copies, row_copies, finish_late, finish_early):
        weight = w_conv.at[layer]
        products(act, weight, 2, (1, 2))
        products(act, weight, 3, (1, 2))
        edge_part[...] = edges(act, range(2, 6), range(1, 5), zeros)
        for f in (4, 2):
            wait_rows(act, f, row_copies[f])
        own_edges = send_edges(2 * layer, edges(act, range(2, 6), (0, 5), edge_part[...]))
        products(act, weight, 2, (0, 3))
        products(act, weight, 3, (0, 3))
        own_edges[0].wait_recv()
        own_edges[1].wait_recv()
        own_cells = received(2 * layer)
        edge_part[...] = own_cells
        edge_products(own_cells, weight)
        finish_late()
        for i, copy in enumerate(frame_copies):
            copy.wait_recv()
            masked(act, (i, slice(1, 5)), group > 0)
        history_rows = send_rows(act, 0)
        history_part = edges(act, range(2), range(1, 5), zeros)
        products(act, weight, 0, (1, 2))
        products(act, weight, 1, (1, 2))
        wait_rows(act, 0, history_rows)
        history_edges = send_edges(2 * layer + 1, edges(act, range(2), (0, 5), history_part))
        products(act, weight, 0, (0, 3))
        products(act, weight, 1, (0, 3))
        history_edges[0].wait_recv()
        history_edges[1].wait_recv()
        edge_products(
            jnp.where(lane < 24, received(2 * layer + 1), edge_part[...]), weight
        )
        finish_early()

    first(2)
    first(3)
    pl.semaphore_wait(barrier, 6)
    frames1 = send_frames(act1)
    rows1 = {4: send_rows(act1, 4)}
    first(0)
    first(1)
    rows1[2] = send_rows(act1, 2)
    w1_load.wait()
    arrange(w_raw[0], 9, 3, store_conv(0))

    rows2 = {}
    frames2 = []

    def second(t):
        for r in range(4):
            act2[2 + t, 1 + r] = activate(convolved(t, r) + vecs[1], vecs[2], r)

    def second_late():
        second(2)
        second(3)
        frames2.extend(send_frames(act2))
        rows2[4] = send_rows(act2, 4)

    def second_early():
        second(0)
        second(1)
        rows2[2] = send_rows(act2, 2)
        w2_load.wait()
        arrange(w_raw[1], 9, 3, store_conv(1))

    conv_layer(0, act1, frames1, rows1, second_late, second_early)

    block_rows = []

    def third(t):
        for r in range(4):
            total = x_rows[t, r].astype(f32) + (convolved(t, r) + vecs[3])
            block[t, r] = (total * inside(r)).astype(bf16)

    def send_block(t):
        frames = pl.ds(t, 2)
        block_rows.append((t, send(block.at[frames, 0], block.at[frames, 4], up)))

    def third_late():
        third(2)
        third(3)
        send_block(2)
        wd_load.wait()
        arrange(wd_raw[...], 3, 1, store_down)

    def third_early():
        third(0)
        third(1)
        send_block(0)

    conv_layer(1, act2, frames2, rows2, third_late, third_early)

    def block_edges(rows, total):
        for t in range(4):
            for r in rows:
                k = t * 5 + r
                value = block[t, r].astype(f32)
                total = jnp.where(lane == k, value if k == 0 else pltpu.roll(value, k, 1), total)
        return total

    edge_cells = block_edges(range(4), zeros)
    for t, copy in block_rows:
        copy.wait_recv()
        for u in (t, t + 1):
            masked(block, (u, 4), down_ok)
    edge_out[4] = block_edges((4,), edge_cells).astype(bf16)
    corner = send(edge_out.at[4], edge_right.at[4], left)
    for t in range(4):
        operand = jnp.concatenate(
            [block[t, 2 * i : 2 * i + 3].reshape(3 * channels, 128) for i in range(2)], axis=1
        )
        total = jnp.dot(w_down[...], operand, preferred_element_type=f32)
        for i in range(2):
            sums[t, i] = total[:, 128 * i : 128 * i + 128]
    corner.wait_recv()
    cells = jnp.where(right_ok, edge_right[4].astype(f32), 0.0)
    operand = jnp.concatenate(
        [cells] + [pltpu.roll(cells, 128 - dr, 1) for dr in (1, 2)], axis=0
    ).astype(bf16)
    east = jnp.dot(w_down[2 * channels :], operand, preferred_element_type=f32)
    picked = (
        lax.broadcasted_iota(jnp.int32, (256, 128), 0)
        == 2 * lax.broadcasted_iota(jnp.int32, (256, 128), 1)
    ).astype(f32).astype(bf16)
    col_limit = jnp.where(right_ok, 1024, col_count)
    stores = []
    for t in range(4):
        halves = []
        for i in range(2):
            row_limit = jnp.where(down_ok, 1024, row_count)
            limit = jnp.where(2 * i + 2 <= row_limit, col_limit, 0)
            keep = (lane_row + 2 <= limit).astype(f32)
            ends = pltpu.roll(east, 126 - (5 * t + 2 * i), 1)
            total = (
                sums[t, i, :channels]
                + pltpu.roll(sums[t, i, channels : 2 * channels], 127, 1)
                + jnp.where(lane == 126, ends, pltpu.roll(sums[t, i, 2 * channels :], 126, 1))
            )
            halves.append(((total + vecs[4]) * keep).astype(bf16))
        result[t] = jnp.dot(
            jnp.concatenate(halves, axis=1), picked, preferred_element_type=f32
        ).astype(bf16)
        copy = pltpu.make_async_copy(result.at[t], out_hbm.at[t], store_sem.at[t])
        copy.start()
        stores.append(copy)
    for copy in sends:
        copy.wait_send()
    for copy in stores:
        copy.wait()


def per_device(grid_rows, groups, video, links, extents, g1, w1, b1, g2, w2, b2, wd, bd):
    _, frames, channels, slab_rows, slab_cols = video.shape
    x = video.reshape(frames, channels * slab_rows, slab_cols)
    vectors = [v.reshape(1, channels) for v in (g1, b1, g2, b2, bd)]
    g1, b1, g2, b2, bd = vectors
    vmem = pltpu.VMEM
    field = (6, 6, channels, 128)
    out = pl.pallas_call(
        functools.partial(kernel, GRID_COLUMN_COUNT, grid_rows, groups),
        out_shape=jax.ShapeDtypeStruct((frames, channels, 128), bf16),
        in_specs=[pl.BlockSpec(memory_space=pltpu.SMEM)] * 2
        + [pl.BlockSpec(memory_space=pl.ANY)] * 9,
        out_specs=pl.BlockSpec(memory_space=pl.ANY),
        scratch_shapes=[
            vmem((4, channels * 4, 128), bf16),
            vmem((channels * 4, 128), f32),
            vmem((4, 4, channels, 128), bf16),
            vmem((2, channels, 27 * channels), bf16),
            vmem((channels, 9 * channels), bf16),
            vmem((5, 1, channels), f32),
            vmem((5, channels, 128), f32),
            vmem((2, 3 * channels, 9 * channels), bf16),
            vmem((3 * channels, 3 * channels), bf16),
            vmem(field, bf16),
            vmem(field, bf16),
            vmem((4, 5, channels, 128), bf16),
            vmem((4, 4, 3 * channels, 128), f32),
            vmem((channels, 128), f32),
            vmem((channels, 128), f32),
            vmem((5, channels, 128), bf16),
            vmem((4, channels, 128), bf16),
            vmem((5, channels, 128), bf16),
            vmem((4, channels, 128), bf16),
            pltpu.SemaphoreType.DMA((12,)),
            pltpu.SemaphoreType.DMA((COPIES,)),
            pltpu.SemaphoreType.DMA((COPIES,)),
            pltpu.SemaphoreType.DMA((4,)),
        ],
        compiler_params=pltpu.CompilerParams(
            collective_id=0, has_side_effects=True, vmem_limit_bytes=60 * 2**20
        ),
    )(links, extents, x, g1, w1, b1, g2, w2, b2, wd, bd)
    return out[None]


def solution(mesh):
    placed = (P("tile", "tm", None, None, None), P("tile", None), P("tile", None)) + (P(),) * 8
    return jax.shard_map(
        functools.partial(
            per_device, mesh.shape["tile"] // GRID_COLUMN_COUNT, mesh.shape["tm"]
        ),
        mesh=mesh,
        in_specs=placed,
        out_specs=P("tile", "tm", None, None),
        check_vma=False,
    )
```

```python
import functools

import jax
import jax.numpy as jnp
from jax import lax
from jax.experimental import pallas as pl
from jax.experimental.pallas import tpu as pltpu
from jax.sharding import PartitionSpec as P

GRID_COLUMN_COUNT = 8
MESH = pl.DeviceIdType.MESH
norm_eps = 1e-06
f32 = jnp.float32
bf16 = jnp.bfloat16

COPIES = 48


def kernel(
    grid_cols,
    grid_rows,
    groups,
    links,
    extents,
    x_hbm,
    g1_hbm,
    w1_hbm,
    b1_hbm,
    g2_hbm,
    w2_hbm,
    b2_hbm,
    wd_hbm,
    bd_hbm,
    out_hbm,
    x_raw,
    spread,
    x_rows,
    w_raw,
    wd_raw,
    vec_raw,
    vecs,
    w_conv,
    w_down,
    act1,
    act2,
    block,
    sums,
    edge_sum,
    edge_own,
    edge_out,
    edge_side,
    edge_corner,
    edge_on,
    edge_past,
    result,
    load_sem,
    send_sem,
    recv_sem,
    store_sem,
):
    channels = vecs.shape[1]
    tile = lax.axis_index("tile")
    group = lax.axis_index("tm")
    grow, gcol = tile // grid_cols, tile % grid_cols
    def slab(rows, cols):
        row = (grow + rows + grid_rows) % grid_rows
        return (row * grid_cols + (gcol + cols + grid_cols) % grid_cols, group)

    up, down, left, right = slab(-1, 0), slab(1, 0), slab(0, -1), slab(0, 1)
    up_left, up_right, down_left, down_right = slab(-1, -1), slab(-1, 1), slab(1, -1), slab(1, 1)
    later = (tile, (group + 1) % groups)
    before = (tile, (group + groups - 1) % groups)
    around = (up, down, left, right, up_left, up_right, down_left, down_right, later, before)

    barrier = pltpu.get_barrier_semaphore()
    for device in around:
        pl.semaphore_signal(barrier, inc=1, device_id=device, device_id_type=MESH)

    loads = []

    def load(src, dst):
        copy = pltpu.make_async_copy(src, dst, load_sem.at[len(loads)])
        copy.start()
        loads.append(copy)
        return copy

    x_loads = {t: load(x_hbm.at[t], x_raw.at[t]) for t in (2, 3, 0, 1)}
    vec_loads = [
        load(ref, vec_raw.at[i]) for i, ref in enumerate((g1_hbm, b1_hbm, g2_hbm, b2_hbm, bd_hbm))
    ]
    w1_load = load(w1_hbm, w_raw.at[0])
    w2_load = load(w2_hbm, w_raw.at[1])
    wd_load = load(wd_hbm, wd_raw)

    sends = []

    def send(src, dst, device):
        i = len(sends)
        copy = pltpu.make_async_remote_copy(
            src_ref=src,
            dst_ref=dst,
            send_sem=send_sem.at[i],
            recv_sem=recv_sem.at[i],
            device_id=device,
            device_id_type=MESH,
        )
        copy.start()
        sends.append(copy)
        return copy

    lane = lax.broadcasted_iota(jnp.int32, (channels, 128), 1)
    lane_row = lax.broadcasted_iota(jnp.int32, (1, 128), 1)
    up_ok, down_ok = links[0, 0] >= 0, links[0, 1] >= 0
    left_ok, right_ok = links[0, 2] >= 0, links[0, 3] >= 0
    row_count, col_count = extents[0, 0], extents[0, 1]

    def inside(r):
        cols = jnp.where(r < row_count, col_count, 0)
        return (lane_row < cols).astype(f32)

    def activate(values, gain, r):
        mean_square = jnp.mean(values * values, axis=0, keepdims=True)
        normed = values * lax.rsqrt(mean_square + norm_eps) * gain
        return (normed / (1.0 + jnp.exp(-normed)) * inside(r)).astype(bf16)

    for copy in vec_loads:
        copy.wait()
    diagonal = lax.broadcasted_iota(jnp.int32, (channels, channels), 0) == lax.broadcasted_iota(
        jnp.int32, (channels, channels), 1
    )
    for i in range(5):
        column = jnp.sum(jnp.where(diagonal, vec_raw[i], 0.0), axis=1, keepdims=True)
        vecs[i] = jnp.broadcast_to(column, (channels, 128))

    def first(t):
        x_loads[t].wait()
        spread[...] = x_raw[t].astype(f32)
        gain = vecs[0]
        for r in range(4):
            values = spread[pl.ds(r, channels, stride=4), :]
            x_rows[t, r] = values.astype(bf16)
            act1[2 + t, 1 + r] = activate(values, gain, r)

    def masked(ref, index, ok):
        ref[index] = jnp.where(ok, ref[index], jnp.zeros_like(ref[index]))

    def send_rows(act, f):
        frames = pl.ds(f, 2)
        return [
            send(act.at[frames, 4], act.at[frames, 0], down),
            send(act.at[frames, 1], act.at[frames, 5], up),
        ]

    def wait_rows(act, f, copies):
        for copy in copies:
            copy.wait_recv()
        for g in (f, f + 1):
            masked(act, (g, 0), up_ok)
            masked(act, (g, 5), down_ok)

    def send_past_rims(act):
        return [
            send(act.at[pl.ds(4, 2), 0], act.at[pl.ds(0, 2), 0], later),
            send(act.at[pl.ds(4, 2), 5], act.at[pl.ds(0, 2), 5], later),
        ]

    def turned(total):
        pad = jnp.zeros((128 - channels, 128), f32)
        return jnp.concatenate([total, pad], axis=0).T

    def send_edges(act, slot, frames):
        total = jnp.zeros((channels, 128), f32)
        for t in frames:
            for r in range(4):
                k = r * 4 + t
                moved = pltpu.roll(act[2 + t, 1 + r].astype(f32), 2 * k + 1, 1)
                total = jnp.where(lane // 2 == k, moved, total)
        edge_out[slot] = turned(total)[:32].astype(bf16)
        whole, upper, lower = (
            edge_out.at[slot],
            edge_out.at[slot, pl.ds(0, 16)],
            edge_out.at[slot, pl.ds(16, 16)],
        )
        return [
            send(whole, edge_side.at[0, slot], right),
            send(whole, edge_side.at[1, slot], left),
            send(lower, edge_corner.at[0, slot], down_right),
            send(lower, edge_corner.at[1, slot], down_left),
            send(upper, edge_corner.at[2, slot], up_right),
            send(upper, edge_corner.at[3, slot], up_left),
        ]

    def chosen(even, even_ok, odd, odd_ok):
        odd_row = lax.broadcasted_iota(jnp.int32, even.shape, 0) % 2 == 1
        even = jnp.where(even_ok, even.astype(f32), 0.0)
        return jnp.where(odd_row, jnp.where(odd_ok, odd.astype(f32), 0.0), even)

    def sides(slot):
        return chosen(edge_side[0, slot], left_ok, edge_side[1, slot], right_ok)

    def upper_corners(slot):
        return chosen(
            edge_corner[0, slot], up_ok & left_ok, edge_corner[1, slot], up_ok & right_ok
        )[8:]

    def lower_corners(slot):
        return chosen(
            edge_corner[2, slot], down_ok & left_ok, edge_corner[3, slot], down_ok & right_ok
        )[:8]

    def whole_edges(slot):
        return jnp.concatenate([upper_corners(slot), sides(slot), lower_corners(slot)], axis=0)

    def edge_cells(own, past):
        first_half = lax.broadcasted_iota(jnp.int32, (8, 128), 0) < 4
        pieces = []
        for row in range(6):
            mine = pltpu.roll(own[8 * row : 8 * row + 8], 4, 0)
            theirs = 0.0
            if past is not None:
                theirs = pltpu.roll(past[8 * row : 8 * row + 8], 4, 0)
            pieces += [jnp.where(first_half, theirs, mine), jnp.where(first_half, mine, 0.0)]
        pieces.append(jnp.zeros((32, 128), f32))
        return jnp.concatenate(pieces, axis=0).T[:channels]

    def patches(act, t, r):
        return jnp.concatenate(
            [act[t + dt, r : r + 3].reshape(3 * channels, 128) for dt in range(3)], axis=0
        )

    def products(act, weight, t, rows):
        operand = jnp.concatenate([patches(act, t, r) for r in rows], axis=1)
        total = jnp.dot(weight[...], operand, preferred_element_type=f32)
        for i, r in enumerate(rows):
            sums[t, r] = total[:, 128 * i : 128 * i + 128]

    def edge_products(cells, weight):
        operand = jnp.concatenate(
            [
                cells if dt + dr == 0 else pltpu.roll(cells, 128 - (16 * dr + 2 * dt), 1)
                for dt in range(3)
                for dr in range(3)
            ],
            axis=0,
        ).astype(bf16)
        west = jnp.dot(weight[:channels], operand, preferred_element_type=f32)
        east = jnp.dot(weight[2 * channels :], operand, preferred_element_type=f32)
        edge_sum[...] = jnp.where(
            lane % 2 == 1, pltpu.roll(west, 1, 1), pltpu.roll(east, 127, 1)
        )

    def convolved(t, r):
        k = 16 * r + 2 * t
        ends = pltpu.roll(edge_sum[...], 128 - (k + 1), 1)
        west = jnp.where(lane == 0, ends, pltpu.roll(sums[t, r, :channels], 1, 1))
        east = jnp.where(lane == 127, ends, pltpu.roll(sums[t, r, 2 * channels :], 127, 1))
        return west + sums[t, r, channels : 2 * channels] + east

    def arrange(raw, taps, step, store):
        value = raw.astype(f32)
        for dc in range(3):
            parts = [
                value[:, (3 * tap + dc) * channels : (3 * tap + dc + 1) * channels]
                for tap in range(taps)
            ]
            store(dc, jnp.concatenate(parts, axis=1).astype(bf16))

    def store_conv(i):
        def put(dc, rows):
            w_conv[i, dc * channels : (dc + 1) * channels] = rows

        return put

    def store_down(dc, rows):
        w_down[dc * channels : (dc + 1) * channels] = rows

    def second(t, rows):
        for r in rows:
            act2[2 + t, 1 + r] = activate(convolved(t, r) + vecs[1], vecs[2], r)

    def third(t):
        for r in range(4):
            total = x_rows[t, r].astype(f32) + (convolved(t, r) + vecs[3])
            block[t, r] = (total * inside(r)).astype(bf16)

    late, early, middle, outer = (2, 3), (0, 1), (1, 2), (0, 3)
    past_frames = pl.ds(0, 2)
    new_frames = pl.ds(4, 2)

    for t in (2, 3, 0, 1):
        first(t)
    w1_load.wait()
    arrange(w_raw[0], 9, 3, store_conv(0))
    pl.semaphore_wait(barrier, len(around))

    edges1 = send_edges(act1, 0, range(4))
    rows1 = send_rows(act1, 4) + send_rows(act1, 2)
    past1 = [
        send(act1.at[4, pl.ds(1, 4)], act1.at[0, pl.ds(1, 4)], later),
        send(act1.at[5, pl.ds(1, 4)], act1.at[1, pl.ds(1, 4)], later),
    ]
    weight1, weight2 = w_conv.at[0], w_conv.at[1]

    for t in late:
        products(act1, weight1, t, middle)
    for copy in edges1[:2]:
        copy.wait_recv()
    no_rows = jnp.zeros((8, 128), f32)
    edge_products(
        edge_cells(jnp.concatenate([no_rows, sides(0), no_rows], axis=0), None), weight1
    )
    for t in late:
        second(t, middle)
    past2 = [send(act2.at[new_frames, pl.ds(2, 2)], act2.at[past_frames, pl.ds(2, 2)], later)]
    wait_rows(act1, 4, rows1[:2])
    past1 += send_past_rims(act1)
    wait_rows(act1, 2, rows1[2:])
    for copy in edges1[2:]:
        copy.wait_recv()
    own = whole_edges(0)
    edge_own[...] = own
    edge_on[0] = own.astype(bf16)
    past1.append(send(edge_on.at[0], edge_past.at[0], later))
    for t in late:
        products(act1, weight1, t, outer)
    edge_products(edge_cells(own, None), weight1)
    for t in late:
        second(t, outer)
    past2 += [
        send(act2.at[new_frames, 1], act2.at[past_frames, 1], later),
        send(act2.at[new_frames, 4], act2.at[past_frames, 4], later),
    ]
    rows2 = send_rows(act2, 4)
    edges2 = send_edges(act2, 1, late)
    w2_load.wait()
    arrange(w_raw[1], 9, 3, store_conv(1))
    wd_load.wait()
    arrange(wd_raw[...], 3, 1, store_down)
    wait_rows(act2, 4, rows2)
    past2 += send_past_rims(act2)
    for copy in edges2:
        copy.wait_recv()
    late_edges = whole_edges(1)
    edge_on[1] = late_edges.astype(bf16)
    past2.append(send(edge_on.at[1], edge_past.at[1], later))

    def take_past(act, copies):
        for copy in copies:
            copy.wait_recv()
        for f in (0, 1):
            masked(act, f, group > 0)

    def past_edges(layer):
        return jnp.where(group > 0, edge_past[layer].astype(f32), 0.0)

    take_past(act1, past1)
    for t in early:
        products(act1, weight1, t, middle)
        products(act1, weight1, t, outer)
    edge_products(edge_cells(edge_own[...], past_edges(0)), weight1)
    edge_own[...] = late_edges
    for t in early:
        second(t, range(4))
    rows2 = send_rows(act2, 2)
    edges2 = send_edges(act2, 2, early)

    for t in late:
        products(act2, weight2, t, middle)
    wait_rows(act2, 2, rows2)
    for t in late:
        products(act2, weight2, t, outer)
    for copy in edges2:
        copy.wait_recv()
    late_row = lax.broadcasted_iota(jnp.int32, (48, 128), 0) % 8 >= 4
    edge_own[...] = jnp.where(late_row, edge_own[...], whole_edges(2))
    take_past(act2, past2)
    for t in early:
        products(act2, weight2, t, middle)
        products(act2, weight2, t, outer)
    edge_products(edge_cells(edge_own[...], past_edges(1)), weight2)
    for t in range(4):
        third(t)
    low_rows = send(block.at[:, 0], block.at[:, 4], up)
    total = jnp.zeros((channels, 128), f32)
    for t in range(4):
        for r in range(4):
            k = r * 4 + t
            value = block[t, r].astype(f32)
            total = jnp.where(lane == k, value if k == 0 else pltpu.roll(value, k, 1), total)
    edge_out[3] = turned(total)[:32].astype(bf16)
    corners = [
        send(edge_out.at[3, pl.ds(0, 16)], edge_side.at[1, 3, pl.ds(0, 16)], left),
        send(edge_out.at[3, pl.ds(0, 16)], edge_corner.at[3, 3], up_left),
    ]
    low_rows.wait_recv()
    for t in range(4):
        masked(block, (t, 4), down_ok)
    for t in range(4):
        operand = jnp.concatenate(
            [block[t, 2 * i : 2 * i + 3].reshape(3 * channels, 128) for i in range(2)], axis=1
        )
        total = jnp.dot(w_down[...], operand, preferred_element_type=f32)
        for i in range(2):
            sums[t, i] = total[:, 128 * i : 128 * i + 128]
    for copy in corners:
        copy.wait_recv()
    cells = jnp.concatenate(
        [
            jnp.where(right_ok, edge_side[1, 3].astype(f32)[:16], 0.0),
            jnp.where(right_ok & down_ok, edge_corner[3, 3].astype(f32)[:8], 0.0),
            jnp.zeros((104, 128), f32),
        ],
        axis=0,
    ).T[:channels]
    operand = jnp.concatenate(
        [cells] + [pltpu.roll(cells, 128 - 4 * dr, 1) for dr in (1, 2)], axis=0
    ).astype(bf16)
    east = jnp.dot(w_down[2 * channels :], operand, preferred_element_type=f32)
    picked = (
        lax.broadcasted_iota(jnp.int32, (256, 128), 0)
        == 2 * lax.broadcasted_iota(jnp.int32, (256, 128), 1)
    ).astype(f32).astype(bf16)
    col_limit = jnp.where(right_ok, 1024, col_count)
    stores = []
    for t in range(4):
        halves = []
        for i in range(2):
            row_limit = jnp.where(down_ok, 1024, row_count)
            limit = jnp.where(2 * i + 2 <= row_limit, col_limit, 0)
            keep = (lane_row + 2 <= limit).astype(f32)
            ends = pltpu.roll(east, 126 - (8 * i + t), 1)
            total = (
                sums[t, i, :channels]
                + pltpu.roll(sums[t, i, channels : 2 * channels], 127, 1)
                + jnp.where(lane == 126, ends, pltpu.roll(sums[t, i, 2 * channels :], 126, 1))
            )
            halves.append(((total + vecs[4]) * keep).astype(bf16))
        result[t] = jnp.dot(
            jnp.concatenate(halves, axis=1), picked, preferred_element_type=f32
        ).astype(bf16)
        copy = pltpu.make_async_copy(result.at[t], out_hbm.at[t], store_sem.at[t])
        copy.start()
        stores.append(copy)
    for copy in sends:
        copy.wait_send()
    for copy in stores:
        copy.wait()


def per_device(grid_rows, groups, video, links, extents, g1, w1, b1, g2, w2, b2, wd, bd):
    _, frames, channels, slab_rows, slab_cols = video.shape
    x = video.reshape(frames, channels * slab_rows, slab_cols)
    vectors = [v.reshape(1, channels) for v in (g1, b1, g2, b2, bd)]
    g1, b1, g2, b2, bd = vectors
    vmem = pltpu.VMEM
    field = (6, 6, channels, 128)
    out = pl.pallas_call(
        functools.partial(kernel, GRID_COLUMN_COUNT, grid_rows, groups),
        out_shape=jax.ShapeDtypeStruct((frames, channels, 128), bf16),
        in_specs=[pl.BlockSpec(memory_space=pltpu.SMEM)] * 2
        + [pl.BlockSpec(memory_space=pl.ANY)] * 9,
        out_specs=pl.BlockSpec(memory_space=pl.ANY),
        scratch_shapes=[
            vmem((4, channels * 4, 128), bf16),
            vmem((channels * 4, 128), f32),
            vmem((4, 4, channels, 128), bf16),
            vmem((2, channels, 27 * channels), bf16),
            vmem((channels, 9 * channels), bf16),
            vmem((5, 1, channels), f32),
            vmem((5, channels, 128), f32),
            vmem((2, 3 * channels, 9 * channels), bf16),
            vmem((3 * channels, 3 * channels), bf16),
            vmem(field, bf16),
            vmem(field, bf16),
            vmem((4, 5, channels, 128), bf16),
            vmem((4, 4, 3 * channels, 128), f32),
            vmem((channels, 128), f32),
            vmem((48, 128), f32),
            vmem((4, 32, 128), bf16),
            vmem((2, 4, 32, 128), bf16),
            vmem((4, 4, 16, 128), bf16),
            vmem((2, 48, 128), bf16),
            vmem((2, 48, 128), bf16),
            vmem((4, channels, 128), bf16),
            pltpu.SemaphoreType.DMA((12,)),
            pltpu.SemaphoreType.DMA((COPIES,)),
            pltpu.SemaphoreType.DMA((COPIES,)),
            pltpu.SemaphoreType.DMA((4,)),
        ],
        compiler_params=pltpu.CompilerParams(
            collective_id=0, has_side_effects=True, vmem_limit_bytes=60 * 2**20
        ),
    )(links, extents, x, g1, w1, b1, g2, w2, b2, wd, bd)
    return out[None]


def solution(mesh):
    placed = (P("tile", "tm", None, None, None), P("tile", None), P("tile", None)) + (P(),) * 8
    return jax.shard_map(
        functools.partial(
            per_device, mesh.shape["tile"] // GRID_COLUMN_COUNT, mesh.shape["tm"]
        ),
        mesh=mesh,
        in_specs=placed,
        out_specs=P("tile", "tm", None, None),
        check_vma=False,
    )
```

```python
import functools

import jax
import jax.numpy as jnp
from jax import lax
from jax.experimental import pallas as pl
from jax.experimental.pallas import tpu as pltpu
from jax.sharding import PartitionSpec as P

GRID_COLUMN_COUNT = 8
MESH = pl.DeviceIdType.MESH
norm_eps = 1e-06
f32 = jnp.float32
bf16 = jnp.bfloat16

COPIES = 48


def kernel(
    grid_cols,
    grid_rows,
    groups,
    links_hbm,
    extents_hbm,
    x_hbm,
    g1_hbm,
    w1_hbm,
    b1_hbm,
    g2_hbm,
    w2_hbm,
    b2_hbm,
    wd_hbm,
    bd_hbm,
    out_hbm,
    links,
    extents,
    x_raw,
    spread,
    x_rows,
    w_raw,
    wd_raw,
    vec_raw,
    vecs,
    w_conv,
    w_down,
    act1,
    act2,
    block,
    sums,
    edge_sum,
    edge_own,
    edge_out,
    edge_side,
    edge_corner,
    edge_on,
    edge_past,
    result,
    load_sem,
    send_sem,
    recv_sem,
    store_sem,
):
    channels = vecs.shape[1]
    tile = lax.axis_index("tile")
    group = lax.axis_index("tm")
    grow, gcol = tile // grid_cols, tile % grid_cols
    def slab(rows, cols, groups_on=0):
        row = (grow + rows + grid_rows) % grid_rows
        col = (gcol + cols + grid_cols) % grid_cols
        return (row * grid_cols + col, (group + groups_on + groups) % groups)

    up, down, left, right = slab(-1, 0), slab(1, 0), slab(0, -1), slab(0, 1)
    up_left, up_right, down_left, down_right = slab(-1, -1), slab(-1, 1), slab(1, -1), slab(1, 1)
    later, before = slab(0, 0, 1), slab(0, 0, -1)
    around = (up, down, left, right, up_left, up_right, down_left, down_right, later, before)

    barrier = pltpu.get_barrier_semaphore()
    for device in around:
        pl.semaphore_signal(barrier, inc=1, device_id=device, device_id_type=MESH)

    loads = []

    def load(src, dst):
        copy = pltpu.make_async_copy(src, dst, load_sem.at[len(loads)])
        copy.start()
        loads.append(copy)
        return copy

    x_loads = {t: load(x_hbm.at[t], x_raw.at[t]) for t in (2, 3, 0, 1)}
    vec_loads = [
        load(ref, vec_raw.at[i]) for i, ref in enumerate((g1_hbm, b1_hbm, g2_hbm, b2_hbm, bd_hbm))
    ]
    scalar_loads = [load(links_hbm, links), load(extents_hbm, extents)]
    w1_load = load(w1_hbm, w_raw.at[0])
    w2_load = load(w2_hbm, w_raw.at[1])
    wd_load = load(wd_hbm, wd_raw)

    sends = []

    def send(src, dst, device):
        i = len(sends)
        copy = pltpu.make_async_remote_copy(
            src_ref=src,
            dst_ref=dst,
            send_sem=send_sem.at[i],
            recv_sem=recv_sem.at[i],
            device_id=device,
            device_id_type=MESH,
        )
        copy.start()
        sends.append(copy)
        return copy

    lane = lax.broadcasted_iota(jnp.int32, (channels, 128), 1)
    lane_row = lax.broadcasted_iota(jnp.int32, (1, 128), 1)
    for copy in scalar_loads:
        copy.wait()
    up_ok, down_ok = links[0, 0] >= 0, links[0, 1] >= 0
    left_ok, right_ok = links[0, 2] >= 0, links[0, 3] >= 0
    row_count, col_count = extents[0, 0], extents[0, 1]

    def inside(r):
        cols = jnp.where(r < row_count, col_count, 0)
        return (lane_row < cols).astype(f32)

    def activate(values, gain, r):
        mean_square = jnp.mean(values * values, axis=0, keepdims=True)
        normed = values * lax.rsqrt(mean_square + norm_eps) * gain
        return (normed / (1.0 + jnp.exp(-normed)) * inside(r)).astype(bf16)

    diagonal = lax.broadcasted_iota(jnp.int32, (channels, channels), 0) == lax.broadcasted_iota(
        jnp.int32, (channels, channels), 1
    )

    def spread_vector(i):
        vec_loads[i].wait()
        column = jnp.sum(jnp.where(diagonal, vec_raw[i], 0.0), axis=1, keepdims=True)
        vecs[i] = jnp.broadcast_to(column, (channels, 128))

    def first(t):
        x_loads[t].wait()
        spread[...] = x_raw[t].astype(f32)
        gain = vecs[0]
        for r in range(4):
            values = spread[pl.ds(r, channels, stride=4), :]
            x_rows[t, r] = values.astype(bf16)
            act1[2 + t, 1 + r] = activate(values, gain, r)

    def masked(ref, index, ok):
        ref[index] = jnp.where(ok, ref[index], jnp.zeros_like(ref[index]))

    def send_rows(act, f):
        frames = pl.ds(f, 2)
        return [
            send(act.at[frames, 4], act.at[frames, 0], down),
            send(act.at[frames, 1], act.at[frames, 5], up),
        ]

    def wait_rows(act, f, copies):
        for copy in copies:
            copy.wait_recv()
        for g in (f, f + 1):
            masked(act, (g, 0), up_ok)
            masked(act, (g, 5), down_ok)

    def send_past_row(act, row):
        return send(act.at[new_frames, row], act.at[past_frames, row], later)

    def send_past_middle(act):
        return send(act.at[new_frames, pl.ds(2, 2)], act.at[past_frames, pl.ds(2, 2)], later)

    def turned(total):
        pad = jnp.zeros((128 - channels, 128), f32)
        return jnp.concatenate([total, pad], axis=0).T

    def send_edges(act, slot, frames):
        total = jnp.zeros((channels, 128), f32)
        for t in frames:
            for r in range(4):
                k = r * 4 + t
                moved = pltpu.roll(act[2 + t, 1 + r].astype(f32), 2 * k + 1, 1)
                total = jnp.where(lane // 2 == k, moved, total)
        edge_out[slot] = turned(total)[:32].astype(bf16)
        whole, upper, lower = (
            edge_out.at[slot],
            edge_out.at[slot, pl.ds(0, 16)],
            edge_out.at[slot, pl.ds(16, 16)],
        )
        return [
            send(whole, edge_side.at[0, slot], right),
            send(whole, edge_side.at[1, slot], left),
            send(lower, edge_corner.at[0, slot], down_right),
            send(lower, edge_corner.at[1, slot], down_left),
            send(upper, edge_corner.at[2, slot], up_right),
            send(upper, edge_corner.at[3, slot], up_left),
        ]

    def chosen(even, even_ok, odd, odd_ok):
        odd_row = lax.broadcasted_iota(jnp.int32, even.shape, 0) % 2 == 1
        even = jnp.where(even_ok, even.astype(f32), 0.0)
        return jnp.where(odd_row, jnp.where(odd_ok, odd.astype(f32), 0.0), even)

    def sides(slot):
        return chosen(edge_side[0, slot], left_ok, edge_side[1, slot], right_ok)

    def upper_corners(slot):
        return chosen(
            edge_corner[0, slot], up_ok & left_ok, edge_corner[1, slot], up_ok & right_ok
        )[8:]

    def lower_corners(slot):
        return chosen(
            edge_corner[2, slot], down_ok & left_ok, edge_corner[3, slot], down_ok & right_ok
        )[:8]

    def whole_edges(slot):
        return jnp.concatenate([upper_corners(slot), sides(slot), lower_corners(slot)], axis=0)

    def edge_cells(own, past):
        first_half = lax.broadcasted_iota(jnp.int32, (8, 128), 0) < 4
        pieces = []
        for row in range(6):
            mine = pltpu.roll(own[8 * row : 8 * row + 8], 4, 0)
            theirs = 0.0
            if past is not None:
                theirs = pltpu.roll(past[8 * row : 8 * row + 8], 4, 0)
            pieces += [jnp.where(first_half, theirs, mine), jnp.where(first_half, mine, 0.0)]
        pieces.append(jnp.zeros((32, 128), f32))
        return jnp.concatenate(pieces, axis=0).T[:channels]

    def patches(act, t, r):
        return jnp.concatenate(
            [act[t + dt, r : r + 3].reshape(3 * channels, 128) for dt in range(3)], axis=0
        )

    def products(act, weight, t, rows):
        operand = jnp.concatenate([patches(act, t, r) for r in rows], axis=1)
        total = jnp.dot(weight[...], operand, preferred_element_type=f32)
        for i, r in enumerate(rows):
            sums[t, r] = total[:, 128 * i : 128 * i + 128]

    def edge_products(cells, weight):
        operand = jnp.concatenate(
            [
                cells if dt + dr == 0 else pltpu.roll(cells, 128 - (16 * dr + 2 * dt), 1)
                for dt in range(3)
                for dr in range(3)
            ],
            axis=0,
        ).astype(bf16)
        west = jnp.dot(weight[:channels], operand, preferred_element_type=f32)
        east = jnp.dot(weight[2 * channels :], operand, preferred_element_type=f32)
        edge_sum[...] = jnp.where(
            lane % 2 == 1, pltpu.roll(west, 1, 1), pltpu.roll(east, 127, 1)
        )

    def convolved(t, r):
        k = 16 * r + 2 * t
        ends = pltpu.roll(edge_sum[...], 128 - (k + 1), 1)
        west = jnp.where(lane == 0, ends, pltpu.roll(sums[t, r, :channels], 1, 1))
        east = jnp.where(lane == 127, ends, pltpu.roll(sums[t, r, 2 * channels :], 127, 1))
        return west + sums[t, r, channels : 2 * channels] + east

    def arrange(raw, taps, step, store):
        value = raw.astype(f32)
        for dc in range(3):
            parts = [
                value[:, (3 * tap + dc) * channels : (3 * tap + dc + 1) * channels]
                for tap in range(taps)
            ]
            store(dc, jnp.concatenate(parts, axis=1).astype(bf16))

    def store_conv(i):
        def put(dc, rows):
            w_conv[i, dc * channels : (dc + 1) * channels] = rows

        return put

    def store_down(dc, rows):
        w_down[dc * channels : (dc + 1) * channels] = rows

    def second(t, rows):
        for r in rows:
            act2[2 + t, 1 + r] = activate(convolved(t, r) + vecs[1], vecs[2], r)

    def third(t):
        for r in range(4):
            total = x_rows[t, r].astype(f32) + (convolved(t, r) + vecs[3])
            block[t, r] = (total * inside(r)).astype(bf16)

    late, early, middle, outer = (2, 3), (0, 1), (1, 2), (0, 3)
    past_frames = pl.ds(0, 2)
    new_frames = pl.ds(4, 2)
    weight1, weight2 = w_conv.at[0], w_conv.at[1]

    def take_past_outer(act, copies):
        for copy in copies:
            copy.wait_recv()
        for f in (0, 1):
            for row in (1, 4):
                masked(act, (f, row), group > 0)
        return send_rows(act, 0)

    def take_past_middle(act, copy):
        copy.wait_recv()
        for f in (0, 1):
            masked(act, (f, slice(2, 4)), group > 0)

    def past_edges(layer):
        return jnp.where(group > 0, edge_past[layer].astype(f32), 0.0)

    def send_past_edges(layer, cells):
        edge_on[layer] = cells.astype(bf16)
        return send(edge_on.at[layer], edge_past.at[layer], later)

    spread_vector(0)
    for t in (2, 3, 0, 1):
        first(t)
    pl.semaphore_wait(barrier, len(around))

    rows1 = send_rows(act1, 4) + send_rows(act1, 2)
    outer1 = [send_past_row(act1, 1), send_past_row(act1, 4)]
    edges1 = send_edges(act1, 0, range(4))
    middle1 = send_past_middle(act1)
    w1_load.wait()
    arrange(w_raw[0], 9, 3, store_conv(0))
    for i in range(1, 5):
        spread_vector(i)

    for t in late:
        products(act1, weight1, t, middle)
    for copy in edges1[:2]:
        copy.wait_recv()
    no_rows = jnp.zeros((8, 128), f32)
    edge_products(
        edge_cells(jnp.concatenate([no_rows, sides(0), no_rows], axis=0), None), weight1
    )
    for t in late:
        second(t, middle)
    middle2 = send_past_middle(act2)
    rims1 = take_past_outer(act1, outer1)
    for copy in edges1[2:]:
        copy.wait_recv()
    own = whole_edges(0)
    edge_own[...] = own
    past_edges1 = send_past_edges(0, own)
    wait_rows(act1, 4, rows1[:2])
    wait_rows(act1, 2, rows1[2:])
    for t in late:
        products(act1, weight1, t, outer)
    edge_products(edge_cells(own, None), weight1)
    for t in late:
        second(t, outer)
    outer2 = [send_past_row(act2, 1), send_past_row(act2, 4)]
    rows2_late = send_rows(act2, 4)
    edges2_late = send_edges(act2, 1, late)

    take_past_middle(act1, middle1)
    for t in early:
        products(act1, weight1, t, middle)
    w2_load.wait()
    arrange(w_raw[1], 9, 3, store_conv(1))
    wait_rows(act1, 0, rims1)
    for t in early:
        products(act1, weight1, t, outer)
    past_edges1.wait_recv()
    edge_products(edge_cells(edge_own[...], past_edges(0)), weight1)
    for t in early:
        second(t, range(4))
    rows2_early = send_rows(act2, 2)
    edges2_early = send_edges(act2, 2, early)
    for copy in edges2_late:
        copy.wait_recv()
    late_edges = whole_edges(1)
    past_edges2 = send_past_edges(1, late_edges)
    edge_own[...] = late_edges
    rims2 = take_past_outer(act2, outer2)
    wd_load.wait()
    arrange(wd_raw[...], 3, 1, store_down)

    for t in late:
        products(act2, weight2, t, middle)
    take_past_middle(act2, middle2)
    for t in early:
        products(act2, weight2, t, middle)
    wait_rows(act2, 4, rows2_late)
    wait_rows(act2, 2, rows2_early)
    for t in late:
        products(act2, weight2, t, outer)
    for copy in edges2_early:
        copy.wait_recv()
    late_row = lax.broadcasted_iota(jnp.int32, (48, 128), 0) % 8 >= 4
    edge_own[...] = jnp.where(late_row, edge_own[...], whole_edges(2))
    edge_products(edge_cells(edge_own[...], None), weight2)
    for t in late:
        third(t)
    low_late = send(block.at[pl.ds(2, 2), 0], block.at[pl.ds(2, 2), 4], up)
    wait_rows(act2, 0, rims2)
    for t in early:
        products(act2, weight2, t, outer)
    past_edges2.wait_recv()
    edge_products(edge_cells(edge_own[...], past_edges(1)), weight2)
    for t in early:
        third(t)
    low_early = send(block.at[pl.ds(0, 2), 0], block.at[pl.ds(0, 2), 4], up)
    total = jnp.zeros((channels, 128), f32)
    for t in range(4):
        for r in range(4):
            k = r * 4 + t
            value = block[t, r].astype(f32)
            total = jnp.where(lane == k, value if k == 0 else pltpu.roll(value, k, 1), total)
    edge_out[3] = turned(total)[:32].astype(bf16)
    corners = [
        send(edge_out.at[3, pl.ds(0, 16)], edge_side.at[1, 3, pl.ds(0, 16)], left),
        send(edge_out.at[3, pl.ds(0, 16)], edge_corner.at[3, 3], up_left),
    ]
    low_late.wait_recv()
    low_early.wait_recv()
    for t in range(4):
        masked(block, (t, 4), down_ok)
    for t in range(4):
        operand = jnp.concatenate(
            [block[t, 2 * i : 2 * i + 3].reshape(3 * channels, 128) for i in range(2)], axis=1
        )
        total = jnp.dot(w_down[...], operand, preferred_element_type=f32)
        for i in range(2):
            sums[t, i] = total[:, 128 * i : 128 * i + 128]
    for copy in corners:
        copy.wait_recv()
    cells = jnp.concatenate(
        [
            jnp.where(right_ok, edge_side[1, 3].astype(f32)[:16], 0.0),
            jnp.where(right_ok & down_ok, edge_corner[3, 3].astype(f32)[:8], 0.0),
            jnp.zeros((104, 128), f32),
        ],
        axis=0,
    ).T[:channels]
    operand = jnp.concatenate(
        [cells] + [pltpu.roll(cells, 128 - 4 * dr, 1) for dr in (1, 2)], axis=0
    ).astype(bf16)
    east = jnp.dot(w_down[2 * channels :], operand, preferred_element_type=f32)
    picked = (
        lax.broadcasted_iota(jnp.int32, (256, 128), 0)
        == 2 * lax.broadcasted_iota(jnp.int32, (256, 128), 1)
    ).astype(f32).astype(bf16)
    col_limit = jnp.where(right_ok, 1024, col_count)
    stores = []
    for t in range(4):
        halves = []
        for i in range(2):
            row_limit = jnp.where(down_ok, 1024, row_count)
            limit = jnp.where(2 * i + 2 <= row_limit, col_limit, 0)
            keep = (lane_row + 2 <= limit).astype(f32)
            ends = pltpu.roll(east, 126 - (8 * i + t), 1)
            total = (
                sums[t, i, :channels]
                + pltpu.roll(sums[t, i, channels : 2 * channels], 127, 1)
                + jnp.where(lane == 126, ends, pltpu.roll(sums[t, i, 2 * channels :], 126, 1))
            )
            halves.append(((total + vecs[4]) * keep).astype(bf16))
        result[t] = jnp.dot(
            jnp.concatenate(halves, axis=1), picked, preferred_element_type=f32
        ).astype(bf16)
        copy = pltpu.make_async_copy(result.at[t], out_hbm.at[t], store_sem.at[t])
        copy.start()
        stores.append(copy)
    for copy in sends:
        copy.wait_send()
    for copy in stores:
        copy.wait()


def per_device(grid_rows, groups, video, links, extents, g1, w1, b1, g2, w2, b2, wd, bd):
    _, frames, channels, slab_rows, slab_cols = video.shape
    x = video.reshape(frames, channels * slab_rows, slab_cols)
    vectors = [v.reshape(1, channels) for v in (g1, b1, g2, b2, bd)]
    g1, b1, g2, b2, bd = vectors
    vmem = pltpu.VMEM
    field = (6, 6, channels, 128)
    out = pl.pallas_call(
        functools.partial(kernel, GRID_COLUMN_COUNT, grid_rows, groups),
        out_shape=jax.ShapeDtypeStruct((frames, channels, 128), bf16),
        in_specs=[pl.BlockSpec(memory_space=pl.ANY)] * 11,
        out_specs=pl.BlockSpec(memory_space=pl.ANY),
        scratch_shapes=[
            pltpu.SMEM((1, 4), jnp.int32),
            pltpu.SMEM((1, 2), jnp.int32),
            vmem((4, channels * 4, 128), bf16),
            vmem((channels * 4, 128), f32),
            vmem((4, 4, channels, 128), bf16),
            vmem((2, channels, 27 * channels), bf16),
            vmem((channels, 9 * channels), bf16),
            vmem((5, 1, channels), f32),
            vmem((5, channels, 128), f32),
            vmem((2, 3 * channels, 9 * channels), bf16),
            vmem((3 * channels, 3 * channels), bf16),
            vmem(field, bf16),
            vmem(field, bf16),
            vmem((4, 5, channels, 128), bf16),
            vmem((4, 4, 3 * channels, 128), f32),
            vmem((channels, 128), f32),
            vmem((48, 128), f32),
            vmem((4, 32, 128), bf16),
            vmem((2, 4, 32, 128), bf16),
            vmem((4, 4, 16, 128), bf16),
            vmem((2, 48, 128), bf16),
            vmem((2, 48, 128), bf16),
            vmem((4, channels, 128), bf16),
            pltpu.SemaphoreType.DMA((14,)),
            pltpu.SemaphoreType.DMA((COPIES,)),
            pltpu.SemaphoreType.DMA((COPIES,)),
            pltpu.SemaphoreType.DMA((4,)),
        ],
        compiler_params=pltpu.CompilerParams(
            collective_id=0, has_side_effects=True, vmem_limit_bytes=60 * 2**20
        ),
    )(links, extents, x, g1, w1, b1, g2, w2, b2, wd, bd)
    return out[None]


def solution(mesh):
    placed = (P("tile", "tm", None, None, None), P("tile", None), P("tile", None)) + (P(),) * 8
    return jax.shard_map(
        functools.partial(
            per_device, mesh.shape["tile"] // GRID_COLUMN_COUNT, mesh.shape["tm"]
        ),
        mesh=mesh,
        in_specs=placed,
        out_specs=P("tile", "tm", None, None),
        check_vma=False,
    )
```

```python
import functools

import jax
import jax.numpy as jnp
from jax import lax
from jax.experimental import pallas as pl
from jax.experimental.pallas import tpu as pltpu
from jax.sharding import PartitionSpec as P

GRID_COLUMN_COUNT = 8
MESH = pl.DeviceIdType.MESH
norm_eps = 1e-06
f32 = jnp.float32
bf16 = jnp.bfloat16

COPIES = 48


def kernel(
    grid_cols,
    grid_rows,
    groups,
    links_hbm,
    extents_hbm,
    x_hbm,
    g1_hbm,
    w1_hbm,
    b1_hbm,
    g2_hbm,
    w2_hbm,
    b2_hbm,
    wd_hbm,
    bd_hbm,
    out_hbm,
    links,
    extents,
    x_raw,
    spread,
    x_rows,
    w_raw,
    wd_raw,
    vec_raw,
    vecs,
    w_conv,
    w_down,
    x_low,
    act1,
    act2,
    block,
    sums,
    edge_sum,
    column_sum,
    pick1,
    pick2,
    edge_own,
    edge_out,
    edge_side,
    edge_corner,
    edge_on,
    edge_past,
    result,
    load_sem,
    send_sem,
    recv_sem,
    store_sem,
):
    channels = vecs.shape[1]
    tile = lax.axis_index("tile")
    group = lax.axis_index("tm")
    grow, gcol = tile // grid_cols, tile % grid_cols
    up, down, left, right = (-1, 0, 0), (1, 0, 0), (0, -1, 0), (0, 1, 0)
    up_left, up_right, down_left, down_right = (-1, -1, 0), (-1, 1, 0), (1, -1, 0), (1, 1, 0)
    later, before = (0, 0, 1), (0, 0, -1)
    around = (up, down, left, right, up_left, up_right, down_left, down_right, later, before)

    def device_at(step):
        row = (grow + step[0] + grid_rows) % grid_rows
        col = (gcol + step[1] + grid_cols) % grid_cols
        return (row * grid_cols + col, (group + step[2] + groups) % groups)

    def is_there(step):
        there = None
        for at, move, size in zip((grow, gcol, group), step, (grid_rows, grid_cols, groups)):
            if move:
                ok = at + move >= 0 if move < 0 else at + move < size
                there = ok if there is None else there & ok
        return there

    there = {step: is_there(step) for step in around}

    barrier = pltpu.get_barrier_semaphore()
    for step in around:

        @pl.when(there[step])
        def _(step=step):
            pl.semaphore_signal(
                barrier, inc=1, device_id=device_at(step), device_id_type=MESH
            )

    loads = []

    def load(src, dst):
        copy = pltpu.make_async_copy(src, dst, load_sem.at[len(loads)])
        copy.start()
        loads.append(copy)
        return copy

    x_loads = {t: load(x_hbm.at[t], x_raw.at[t]) for t in (2, 3, 0, 1)}
    vec_loads = [
        load(ref, vec_raw.at[i]) for i, ref in enumerate((g1_hbm, b1_hbm, g2_hbm, b2_hbm, bd_hbm))
    ]
    scalar_loads = [load(links_hbm, links), load(extents_hbm, extents)]
    w1_load = load(w1_hbm, w_raw.at[0])
    w2_load = load(w2_hbm, w_raw.at[1])
    wd_load = load(wd_hbm, wd_raw)

    sends = []

    def send(src, dst, step):
        i = len(sends)
        copy = pltpu.make_async_remote_copy(
            src_ref=src,
            dst_ref=dst,
            send_sem=send_sem.at[i],
            recv_sem=recv_sem.at[i],
            device_id=device_at(step),
            device_id_type=MESH,
        )
        pl.when(there[step])(copy.start)
        sends.append((copy, there[step]))
        return copy, there[tuple(-move for move in step)]

    def arrive(*copies):
        for copy, ok in copies:
            pl.when(ok)(copy.wait_recv)

    lane = lax.broadcasted_iota(jnp.int32, (channels, 128), 1)
    lane_row = lax.broadcasted_iota(jnp.int32, (1, 128), 1)
    for copy in scalar_loads:
        copy.wait()
    up_ok, down_ok = links[0, 0] >= 0, links[0, 1] >= 0
    left_ok, right_ok = links[0, 2] >= 0, links[0, 3] >= 0
    row_count, col_count = extents[0, 0], extents[0, 1]

    def inside(r):
        cols = jnp.where(r < row_count, col_count, 0)
        return (lane_row < cols).astype(f32)

    def activate(values, gain, r):
        mean_square = jnp.mean(values * values, axis=0, keepdims=True)
        normed = values * lax.rsqrt(mean_square + norm_eps) * gain
        return (normed / (1.0 + jnp.exp(-normed)) * inside(r)).astype(bf16)

    diagonal = lax.broadcasted_iota(jnp.int32, (channels, channels), 0) == lax.broadcasted_iota(
        jnp.int32, (channels, channels), 1
    )

    def spread_vector(i):
        vec_loads[i].wait()
        column = jnp.sum(jnp.where(diagonal, vec_raw[i], 0.0), axis=1, keepdims=True)
        vecs[i] = jnp.broadcast_to(column, (channels, 128))

    def first(t):
        x_loads[t].wait()
        spread[...] = x_raw[t].astype(f32)
        gain = vecs[0]
        for r in range(4):
            values = spread[pl.ds(r, channels, stride=4), :]
            x_rows[t, r] = values.astype(bf16)
            act1[2 + t, 1 + r] = activate(values, gain, r)

    def masked(ref, index, ok):
        ref[index] = jnp.where(ok, ref[index], jnp.zeros_like(ref[index]))

    def send_rows(act, f):
        frames = pl.ds(f, 2)
        copies = [
            send(act.at[frames, 4], act.at[frames, 0], down),
            send(act.at[frames, 1], act.at[frames, 5], up),
        ]
        if act.shape[1] > 6:
            copies.append(send(act.at[frames, 2], act.at[frames, 6], up))
        return copies

    def wait_rows(act, f, copies):
        arrive(*copies[:2])
        for g in (f, f + 1):
            masked(act, (g, 0), up_ok)
            masked(act, (g, 5), down_ok)

    def wait_low_row(act, f, copies):
        arrive(copies[2])
        for g in (f, f + 1):
            masked(act, (g, 6), down_ok)

    def send_past_row(act, row):
        return send(act.at[new_frames, row], act.at[past_frames, row], later)

    def send_past_middle(act):
        return send(act.at[new_frames, pl.ds(2, 2)], act.at[past_frames, pl.ds(2, 2)], later)

    pick_row = lax.broadcasted_iota(jnp.int32, (64, 128), 0)
    pick_lane = lax.broadcasted_iota(jnp.int32, (64, 128), 1)

    def picks(*pairs):
        hit = False
        for row, col in pairs:
            hit = hit | ((pick_row == row) & (pick_lane == col))
        return jnp.where(hit, 1.0, 0.0).astype(bf16)

    def edge_row(t, r):
        return r // 2 * 32 + r % 2 * 8 + t * 2

    def fill_picks(ref, *wanted):
        for i, pairs in enumerate(wanted):
            for t in range(4):
                for r in range(4):
                    at = ((i * 4 + t) * 4 + r) * 128
                    ref[:, at : at + 128] = picks(
                        *[(edge_row(t, r) + row, col) for row, col in pairs]
                    )

    def gather_edges(slot, pick, cells):
        rows = lax.dot_general(
            pick,
            jnp.concatenate(cells, axis=1),
            (((1,), (1,)), ((), ())),
            preferred_element_type=f32,
        )
        edge_out[slot, :, :channels] = rows.astype(bf16)
        edge_out[slot, :, channels:] = jnp.zeros((64, 128 - channels), bf16)

    def gather_edges2(slot, frames):
        cells = [act2[2 + t, 1 + r] for t in frames for r in range(4)]
        gather_edges(slot, pick2[:, frames[0] * 512 : frames[0] * 512 + 1024], cells)
        return send_edges(slot)

    def send_edges(slot):
        whole, upper, lower = (
            edge_out.at[slot],
            edge_out.at[slot, pl.ds(0, 32)],
            edge_out.at[slot, pl.ds(32, 32)],
        )
        copies = [
            send(whole, edge_side.at[0, slot], right),
            send(whole, edge_side.at[1, slot], left),
            send(lower, edge_corner.at[0, slot], down_right),
            send(lower, edge_corner.at[1, slot], down_left),
            send(upper, edge_corner.at[2, slot], up_right),
            send(upper, edge_corner.at[3, slot], up_left),
        ]
        if slot > 0:
            copies += [
                send(lower, edge_corner.at[4, slot], down),
                send(upper, edge_corner.at[5, slot], up),
            ]
        return copies

    def chosen(even, even_ok, odd, odd_ok):
        odd_row = lax.broadcasted_iota(jnp.int32, even.shape, 0) % 2 == 1
        even = jnp.where(even_ok, even, 0.0)
        return jnp.where(odd_row, jnp.where(odd_ok, odd, 0.0), even)

    def whole(value, part):
        value = value.astype(f32)
        return jnp.concatenate(
            [value[16 * part : 16 * part + 16], value[16 * part + 32 : 16 * part + 48]], axis=0
        )

    def above(i, slot, part):
        return edge_corner[i, slot].astype(f32)[16 * part + 8 : 16 * part + 16]

    def below(i, slot, part):
        return edge_corner[i, slot].astype(f32)[16 * part : 16 * part + 16]

    def sides(slot):
        return chosen(
            whole(edge_side[0, slot], 0), left_ok, whole(edge_side[1, slot], 0), right_ok
        )

    def outer_edges(slot):
        upper = chosen(above(0, slot, 0), up_ok & left_ok, above(1, slot, 0), up_ok & right_ok)
        lower = chosen(below(2, slot, 0), down_ok & left_ok, below(3, slot, 0), down_ok & right_ok)
        return jnp.concatenate([upper, sides(slot), lower], axis=0)

    def inner_edges(slot):
        upper = chosen(above(4, slot, 0), up_ok, above(1, slot, 1), up_ok & right_ok)
        middle = chosen(whole(edge_out[slot], 0), True, whole(edge_side[1, slot], 1), right_ok)
        lower = chosen(below(5, slot, 0), down_ok, below(3, slot, 1), down_ok & right_ok)
        return jnp.concatenate([upper, middle, lower], axis=0)

    def edge_cells(own, past):
        first_half = lax.broadcasted_iota(jnp.int32, (8, 128), 0) < 4
        pieces = []
        for row in range(7):
            mine = pltpu.roll(own[8 * row : 8 * row + 8], 4, 0)
            theirs = 0.0
            if past is not None:
                theirs = pltpu.roll(past[8 * row : 8 * row + 8], 4, 0)
            pieces += [jnp.where(first_half, theirs, mine), jnp.where(first_half, mine, 0.0)]
        pieces.append(jnp.zeros((16, 128), f32))
        return jnp.concatenate(pieces, axis=0).T[:channels]

    def patches(act, t, r):
        return jnp.concatenate(
            [act[t + dt, r : r + 3].reshape(3 * channels, 128) for dt in range(3)], axis=0
        )

    def products(act, weight, cells):
        operand = jnp.concatenate([patches(act, t, r) for t, r in cells], axis=1)
        total = jnp.dot(weight[...], operand, preferred_element_type=f32)
        for i, (t, r) in enumerate(cells):
            sums[t, r] = total[:, 128 * i : 128 * i + 128]

    def stacked(cells):
        return jnp.concatenate(
            [
                cells if dt + dr == 0 else pltpu.roll(cells, 128 - (16 * dr + 2 * dt), 1)
                for dt in range(3)
                for dr in range(3)
            ],
            axis=0,
        ).astype(bf16)

    def product(rows, operand):
        return jnp.dot(rows, operand, preferred_element_type=f32)

    def edge_products(cells, weight):
        operand = stacked(cells)
        west = product(weight[:channels], operand)
        east = product(weight[2 * channels :], operand)
        edge_sum[...] = jnp.where(
            lane % 2 == 1, pltpu.roll(west, 1, 1), pltpu.roll(east, 127, 1)
        )

    def column_products(outer_cells, inner_cells, weight):
        both = product(weight[...], stacked(outer_cells))
        west, centre, east = (both[i * channels : (i + 1) * channels] for i in range(3))
        edge_sum[...] = jnp.where(
            lane % 2 == 1, pltpu.roll(west, 1, 1), pltpu.roll(east, 127, 1)
        )
        operand = stacked(inner_cells)
        west = product(weight[:channels], operand)
        east = product(weight[2 * channels :], operand)
        column_sum[...] = centre + east + pltpu.roll(west, 1, 1)

    def convolved(t, r):
        k = 16 * r + 2 * t
        ends = pltpu.roll(edge_sum[...], 128 - (k + 1), 1)
        west = jnp.where(lane == 0, ends, pltpu.roll(sums[t, r, :channels], 1, 1))
        east = jnp.where(lane == 127, ends, pltpu.roll(sums[t, r, 2 * channels :], 127, 1))
        return west + sums[t, r, channels : 2 * channels] + east

    def arrange(raw, taps, step, store):
        value = raw.astype(f32)
        for dc in range(3):
            parts = [
                value[:, (3 * tap + dc) * channels : (3 * tap + dc + 1) * channels]
                for tap in range(taps)
            ]
            store(dc, jnp.concatenate(parts, axis=1).astype(bf16))

    def store_conv(i):
        def put(dc, rows):
            w_conv[i, dc * channels : (dc + 1) * channels] = rows

        return put

    def store_down(dc, rows):
        w_down[dc * channels : (dc + 1) * channels] = rows

    def second(t, rows):
        for r in rows:
            act2[2 + t, 1 + r] = activate(convolved(t, r) + vecs[1], vecs[2], r)

    def third(t):
        for r in range(5):
            residual = x_rows[t, r] if r < 4 else x_low[t]
            total = residual.astype(f32) + (convolved(t, r) + vecs[3])
            ok = inside(r) if r < 4 else low_inside
            block[t, r] = (total * ok).astype(bf16)

    late, early, middle, outer = (2, 3), (0, 1), (1, 2), (0, 3)
    past_frames = pl.ds(0, 2)
    new_frames = pl.ds(4, 2)
    weight1, weight2 = w_conv.at[0], w_conv.at[1]

    def take_past_outer(act, copies):
        arrive(*copies)
        for f in (0, 1):
            for row in (1, 4):
                masked(act, (f, row), group > 0)
        return send_rows(act, 0)

    def take_past_middle(act, copy):
        arrive(copy)
        for f in (0, 1):
            masked(act, (f, slice(2, 4)), group > 0)

    def past_edges(layer, part):
        return jnp.where(group > 0, edge_past[layer, part].astype(f32), 0.0)[:56]

    no_rows = jnp.zeros((8, 128), f32)

    def send_past_edges(layer, parts):
        for i, cells in enumerate(parts):
            edge_on[layer, i] = jnp.concatenate([cells, no_rows], axis=0).astype(bf16)
        some = pl.ds(0, len(parts))
        return send(edge_on.at[layer, some], edge_past.at[layer, some], later)

    spread_vector(0)
    for t in (2, 3, 0, 1):
        first(t)
    fill_picks(pick1, ((0, 127), (1, 0)), ((17, 0),))
    cells = [(t, r) for t in range(4) for r in range(4)]
    gather_edges(
        0, pick1[...], [act1[2 + t, 1 + r] for t, r in cells] + [x_rows[t, r] for t, r in cells]
    )
    pl.semaphore_wait(barrier, sum(there[step].astype(jnp.int32) for step in around))

    outer1 = [send_past_row(act1, 1), send_past_row(act1, 4)]
    edges1 = send_edges(0)
    rows1 = send_rows(act1, 4) + send_rows(act1, 2)
    middle1 = send_past_middle(act1)
    low1 = send(x_rows.at[:, 0], x_low, up)
    w1_load.wait()
    arrange(w_raw[0], 9, 3, store_conv(0))
    for i in range(1, 5):
        spread_vector(i)
    fill_picks(pick2, ((0, 127), (1, 0), (17, 1)))

    for t in late:
        products(act1, weight1, [(t, r) for r in middle])
    arrive(*edges1[:2])
    edge_products(
        edge_cells(jnp.concatenate([no_rows, sides(0), no_rows, no_rows], axis=0), None), weight1
    )
    for t in late:
        second(t, middle)
    middle2 = send_past_middle(act2)
    rims1 = take_past_outer(act1, outer1)
    arrive(*edges1[2:])
    own = outer_edges(0)
    edge_own[0] = own
    past_edges1 = send_past_edges(0, [own])
    wait_rows(act1, 4, rows1[:2])
    wait_rows(act1, 2, rows1[2:])
    for t in late:
        products(act1, weight1, [(t, r) for r in outer])
    edge_products(edge_cells(own, None), weight1)
    for t in late:
        second(t, outer)
    outer2 = [send_past_row(act2, 1), send_past_row(act2, 4)]
    edges2_late = gather_edges2(1, late)
    rows2_late = send_rows(act2, 4)

    take_past_middle(act1, middle1)
    for t in early:
        products(act1, weight1, [(t, r) for r in middle])
    w2_load.wait()
    arrange(w_raw[1], 9, 3, store_conv(1))
    wait_rows(act1, 0, rims1)
    for t in early:
        products(act1, weight1, [(t, r) for r in outer])
    arrive(past_edges1)
    edge_products(edge_cells(edge_own[0], past_edges(0, 0)), weight1)
    for t in early:
        second(t, range(4))
    edges2_early = gather_edges2(2, early)
    rows2_early = send_rows(act2, 2)
    take_past_middle(act2, middle2)
    rims2 = take_past_outer(act2, outer2)
    arrive(*edges2_late)
    edge_own[0] = outer_edges(1)
    edge_own[1] = inner_edges(1)
    past_edges2 = send_past_edges(1, [edge_own[0], edge_own[1]])
    wd_load.wait()
    arrange(wd_raw[...], 3, 1, store_down)

    arrive(low1)
    for t in range(4):
        masked(x_low, t, down_ok)
    low_inside = (lane_row < jnp.where(down_ok, col_count, 0)).astype(f32)
    for t in range(4):
        products(act2, weight2, [(t, r) for r in middle])
    wait_rows(act2, 4, rows2_late)
    wait_rows(act2, 2, rows2_early)
    for t in late:
        products(act2, weight2, [(t, r) for r in outer])
    wait_low_row(act2, 4, rows2_late)
    wait_low_row(act2, 2, rows2_early)
    products(act2, weight2, [(t, 4) for t in late])
    arrive(*edges2_early)
    late_row = lax.broadcasted_iota(jnp.int32, (56, 128), 0) % 8 >= 4
    outer_own = jnp.where(late_row, edge_own[0], outer_edges(2))
    inner_own = jnp.where(late_row, edge_own[1], inner_edges(2))
    arrive(past_edges2)
    column_products(
        edge_cells(outer_own, past_edges(1, 0)), edge_cells(inner_own, past_edges(1, 1)), weight2
    )
    for t in late:
        third(t)
    wait_rows(act2, 0, rims2)
    for t in early:
        products(act2, weight2, [(t, r) for r in outer])
    wait_low_row(act2, 0, rims2)
    products(act2, weight2, [(t, 4) for t in early])
    for t in early:
        third(t)
    x_column = [edge_side[1, 0].astype(f32)[16:32], edge_side[1, 0].astype(f32)[48:64]]
    x_column = [x_column[r // 2][8 * (r % 2) : 8 * (r % 2) + 8] for r in range(4)]
    x_column.append(below(3, 0, 1)[:8])
    x_column = sum([[rows, no_rows] for rows in x_column], []) + [jnp.zeros((48, 128), f32)]
    slab_row = lane // 16
    row_inside = ((slab_row < 4) & (slab_row < row_count)) | ((slab_row == 4) & down_ok)
    cells = jnp.concatenate(x_column, axis=0).T[:channels] + (column_sum[...] + vecs[3])
    cells = jnp.where(row_inside & right_ok, cells, 0.0)
    for t in range(4):
        operand = jnp.concatenate(
            [block[t, 2 * i : 2 * i + 3].reshape(3 * channels, 128) for i in range(2)], axis=1
        )
        total = product(w_down[...], operand)
        for i in range(2):
            sums[t, i] = total[:, 128 * i : 128 * i + 128]
    operand = jnp.concatenate(
        [cells, pltpu.roll(cells, 112, 1), pltpu.roll(cells, 96, 1)], axis=0
    ).astype(bf16)
    east = product(w_down[2 * channels :], operand)
    picked = (
        lax.broadcasted_iota(jnp.int32, (256, 128), 0)
        == 2 * lax.broadcasted_iota(jnp.int32, (256, 128), 1)
    ).astype(f32).astype(bf16)
    col_limit = jnp.where(right_ok, 1024, col_count)
    stores = []
    for t in range(4):
        halves = []
        for i in range(2):
            row_limit = jnp.where(down_ok, 1024, row_count)
            limit = jnp.where(2 * i + 2 <= row_limit, col_limit, 0)
            keep = (lane_row + 2 <= limit).astype(f32)
            ends = pltpu.roll(east, 126 - (32 * i + 2 * t + 1), 1)
            total = (
                sums[t, i, :channels]
                + pltpu.roll(sums[t, i, channels : 2 * channels], 127, 1)
                + jnp.where(lane == 126, ends, pltpu.roll(sums[t, i, 2 * channels :], 126, 1))
            )
            halves.append(((total + vecs[4]) * keep).astype(bf16))
        result[t] = jnp.dot(
            jnp.concatenate(halves, axis=1), picked, preferred_element_type=f32
        ).astype(bf16)
        copy = pltpu.make_async_copy(result.at[t], out_hbm.at[t], store_sem.at[t])
        copy.start()
        stores.append(copy)
    for copy, ok in sends:
        pl.when(ok)(copy.wait_send)
    for copy in stores:
        copy.wait()


def per_device(grid_rows, groups, video, links, extents, g1, w1, b1, g2, w2, b2, wd, bd):
    _, frames, channels, slab_rows, slab_cols = video.shape
    x = video.reshape(frames, channels * slab_rows, slab_cols)
    vectors = [v.reshape(1, channels) for v in (g1, b1, g2, b2, bd)]
    g1, b1, g2, b2, bd = vectors
    vmem = pltpu.VMEM
    out = pl.pallas_call(
        functools.partial(kernel, GRID_COLUMN_COUNT, grid_rows, groups),
        out_shape=jax.ShapeDtypeStruct((frames, channels, 128), bf16),
        in_specs=[pl.BlockSpec(memory_space=pl.ANY)] * 11,
        out_specs=pl.BlockSpec(memory_space=pl.ANY),
        scratch_shapes=[
            pltpu.SMEM((1, 4), jnp.int32),
            pltpu.SMEM((1, 2), jnp.int32),
            vmem((4, channels * 4, 128), bf16),
            vmem((channels * 4, 128), f32),
            vmem((4, 4, channels, 128), bf16),
            vmem((2, channels, 27 * channels), bf16),
            vmem((channels, 9 * channels), bf16),
            vmem((5, 1, channels), f32),
            vmem((5, channels, 128), f32),
            vmem((2, 3 * channels, 9 * channels), bf16),
            vmem((3 * channels, 3 * channels), bf16),
            vmem((4, channels, 128), bf16),
            vmem((6, 6, channels, 128), bf16),
            vmem((6, 7, channels, 128), bf16),
            vmem((4, 5, channels, 128), bf16),
            vmem((4, 5, 3 * channels, 128), f32),
            vmem((channels, 128), f32),
            vmem((channels, 128), f32),
            vmem((64, 32 * 128), bf16),
            vmem((64, 16 * 128), bf16),
            vmem((2, 56, 128), f32),
            vmem((3, 64, 128), bf16),
            vmem((2, 3, 64, 128), bf16),
            vmem((6, 3, 32, 128), bf16),
            vmem((2, 2, 64, 128), bf16),
            vmem((2, 2, 64, 128), bf16),
            vmem((4, channels, 128), bf16),
            pltpu.SemaphoreType.DMA((14,)),
            pltpu.SemaphoreType.DMA((COPIES,)),
            pltpu.SemaphoreType.DMA((COPIES,)),
            pltpu.SemaphoreType.DMA((4,)),
        ],
        compiler_params=pltpu.CompilerParams(
            collective_id=0, has_side_effects=True, vmem_limit_bytes=60 * 2**20
        ),
    )(links, extents, x, g1, w1, b1, g2, w2, b2, wd, bd)
    return out[None]


def solution(mesh):
    placed = (P("tile", "tm", None, None, None), P("tile", None), P("tile", None)) + (P(),) * 8
    return jax.shard_map(
        functools.partial(
            per_device, mesh.shape["tile"] // GRID_COLUMN_COUNT, mesh.shape["tm"]
        ),
        mesh=mesh,
        in_specs=placed,
        out_specs=P("tile", "tm", None, None),
        check_vma=False,
    )
```

```python
import functools

import jax
import jax.numpy as jnp
from jax import lax
from jax.experimental import pallas as pl
from jax.experimental.pallas import tpu as pltpu
from jax.sharding import PartitionSpec as P

GRID_COLUMN_COUNT = 8
MESH = pl.DeviceIdType.MESH
norm_eps = 1e-06
f32 = jnp.float32
bf16 = jnp.bfloat16

COPIES = 64


def kernel(
    grid_cols,
    grid_rows,
    groups,
    links_hbm,
    extents_hbm,
    x_hbm,
    g1_hbm,
    w1_hbm,
    b1_hbm,
    g2_hbm,
    w2_hbm,
    b2_hbm,
    wd_hbm,
    bd_hbm,
    out_hbm,
    links,
    extents,
    x_raw,
    spread,
    x_rows,
    w_raw,
    wd_raw,
    vec_raw,
    vecs,
    w_conv,
    w_edge,
    w_down,
    x_low,
    act1,
    act2,
    block,
    sums,
    edge_sum,
    column_sum,
    pick1,
    pick2,
    edge_own,
    edge_out,
    edge_side,
    edge_corner,
    edge_on,
    edge_past,
    edge_low_on,
    edge_low_past,
    result,
    load_sem,
    send_sem,
    recv_sem,
    store_sem,
):
    channels = vecs.shape[1]
    tile = lax.axis_index("tile")
    group = lax.axis_index("tm")
    grow, gcol = tile // grid_cols, tile % grid_cols
    up, down, left, right = (-1, 0, 0), (1, 0, 0), (0, -1, 0), (0, 1, 0)
    up_left, up_right, down_left, down_right = (-1, -1, 0), (-1, 1, 0), (1, -1, 0), (1, 1, 0)
    later, before = (0, 0, 1), (0, 0, -1)
    around = (up, down, left, right, up_left, up_right, down_left, down_right, later, before)

    def device_at(step):
        row = (grow + step[0] + grid_rows) % grid_rows
        col = (gcol + step[1] + grid_cols) % grid_cols
        return (row * grid_cols + col, (group + step[2] + groups) % groups)

    def is_there(step):
        there = None
        for at, move, size in zip((grow, gcol, group), step, (grid_rows, grid_cols, groups)):
            if move:
                ok = at + move >= 0 if move < 0 else at + move < size
                there = ok if there is None else there & ok
        return there

    there = {step: is_there(step) for step in around}

    barrier = pltpu.get_barrier_semaphore()
    for step in around:

        @pl.when(there[step])
        def _(step=step):
            pl.semaphore_signal(
                barrier, inc=1, device_id=device_at(step), device_id_type=MESH
            )

    loads = []

    def load(src, dst):
        copy = pltpu.make_async_copy(src, dst, load_sem.at[len(loads)])
        copy.start()
        loads.append(copy)
        return copy

    x_loads = {t: load(x_hbm.at[t], x_raw.at[t]) for t in (2, 3, 0, 1)}
    vec_loads = [
        load(ref, vec_raw.at[i]) for i, ref in enumerate((g1_hbm, b1_hbm, g2_hbm, b2_hbm, bd_hbm))
    ]
    scalar_loads = [load(links_hbm, links), load(extents_hbm, extents)]
    w1_load = load(w1_hbm, w_raw.at[0])
    w2_load = load(w2_hbm, w_raw.at[1])
    wd_load = load(wd_hbm, wd_raw)

    sends = []

    def send(src, dst, step):
        i = len(sends)
        copy = pltpu.make_async_remote_copy(
            src_ref=src,
            dst_ref=dst,
            send_sem=send_sem.at[i],
            recv_sem=recv_sem.at[i],
            device_id=device_at(step),
            device_id_type=MESH,
        )
        pl.when(there[step])(copy.start)
        sends.append((copy, there[step]))
        return copy, there[tuple(-move for move in step)]

    def arrive(*copies):
        for copy, ok in copies:
            pl.when(ok)(copy.wait_recv)

    lane = lax.broadcasted_iota(jnp.int32, (channels, 128), 1)
    lane_row = lax.broadcasted_iota(jnp.int32, (1, 128), 1)
    for copy in scalar_loads:
        copy.wait()
    up_ok, down_ok = links[0, 0] >= 0, links[0, 1] >= 0
    left_ok, right_ok = links[0, 2] >= 0, links[0, 3] >= 0
    row_count, col_count = extents[0, 0], extents[0, 1]

    def inside(r):
        cols = jnp.where(r < row_count, col_count, 0)
        return (lane_row < cols).astype(f32)

    def activate(values, gain, r):
        mean_square = jnp.mean(values * values, axis=0, keepdims=True)
        normed = values * lax.rsqrt(mean_square + norm_eps) * gain
        return (normed / (1.0 + jnp.exp(-normed)) * inside(r)).astype(bf16)

    diagonal = lax.broadcasted_iota(jnp.int32, (channels, channels), 0) == lax.broadcasted_iota(
        jnp.int32, (channels, channels), 1
    )

    def spread_vector(i):
        vec_loads[i].wait()
        column = jnp.sum(jnp.where(diagonal, vec_raw[i], 0.0), axis=1, keepdims=True)
        vecs[i] = jnp.broadcast_to(column, (channels, 128))

    def first(t):
        x_loads[t].wait()
        spread[...] = x_raw[t].astype(f32)
        gain = vecs[0]
        for r in range(4):
            values = spread[pl.ds(r, channels, stride=4), :]
            x_rows[t, r] = values.astype(bf16)
            act1[2 + t, 1 + r] = activate(values, gain, r)

    def masked(ref, index, ok):
        ref[index] = jnp.where(ok, ref[index], jnp.zeros_like(ref[index]))

    def send_rows_up(act, f):
        frames = pl.ds(f, 2)
        copies = [send(act.at[frames, 1], act.at[frames, 5], up)]
        if act.shape[1] > 6:
            copies.append(send(act.at[frames, 2], act.at[frames, 6], up))
        return copies

    def send_rows_down(act, f):
        frames = pl.ds(f, 2)
        return send(act.at[frames, 4], act.at[frames, 0], down)

    def send_rows(act, f):
        return [send_rows_down(act, f)] + send_rows_up(act, f)

    def wait_upper(act, f, copies):
        arrive(copies[0])
        for g in (f, f + 1):
            masked(act, (g, 0), up_ok)

    def wait_lower(act, f, copies):
        arrive(copies[1])
        for g in (f, f + 1):
            masked(act, (g, 5), down_ok)

    def wait_low_row(act, f, copies):
        arrive(copies[2])
        for g in (f, f + 1):
            masked(act, (g, 6), down_ok)

    def send_past_row(act, row):
        return send(act.at[new_frames, row], act.at[past_frames, row], later)

    def send_past_middle(act):
        return send(act.at[new_frames, pl.ds(2, 2)], act.at[past_frames, pl.ds(2, 2)], later)

    pick_row = lax.broadcasted_iota(jnp.int32, (64, 128), 0)
    pick_lane = lax.broadcasted_iota(jnp.int32, (64, 128), 1)

    def picks(*pairs):
        hit = False
        for row, col in pairs:
            hit = hit | ((pick_row == row) & (pick_lane == col))
        return jnp.where(hit, 1.0, 0.0).astype(bf16)

    def edge_row(t, r):
        return r // 2 * 32 + r % 2 * 8 + t * 2

    def fill_picks(ref, *wanted):
        for i, pairs in enumerate(wanted):
            for t in range(4):
                for r in range(4):
                    at = ((i * 4 + t) * 4 + r) * 128
                    ref[:, at : at + 128] = picks(
                        *[(edge_row(t, r) + row, col) for row, col in pairs]
                    )

    def gather_edges(slot, pick, cells):
        rows = lax.dot_general(
            pick,
            jnp.concatenate(cells, axis=1),
            (((1,), (1,)), ((), ())),
            preferred_element_type=f32,
        )
        edge_out[slot, :, :channels] = rows.astype(bf16)
        edge_out[slot, :, channels:] = jnp.zeros((64, 128 - channels), bf16)

    def gather_edges2(slot, frames, half):
        mine = pl.ds(32 * half, 32)
        cells = [act2[2 + t, 1 + r] for t in frames for r in (2 * half, 2 * half + 1)]
        pick = jnp.concatenate(
            [pick2[mine, t * 512 + half * 256 : t * 512 + half * 256 + 256] for t in frames],
            axis=1,
        )
        rows = lax.dot_general(
            pick,
            jnp.concatenate(cells, axis=1),
            (((1,), (1,)), ((), ())),
            preferred_element_type=f32,
        )
        edge_out[slot, mine, :channels] = rows.astype(bf16)
        edge_out[slot, mine, channels:] = jnp.zeros((32, 128 - channels), bf16)
        part = edge_out.at[slot, mine]
        first, steps = (
            (2, (up_right, up_left, up)) if half == 0 else (0, (down_right, down_left, down))
        )
        slots = (first, first + 1, 5 if half == 0 else 4)
        return [
            send(part, edge_side.at[0, slot, mine], right),
            send(part, edge_side.at[1, slot, mine], left),
        ] + [send(part, edge_corner.at[i, slot], step) for i, step in zip(slots, steps)]

    def send_edges(slot):
        whole, upper, lower = (
            edge_out.at[slot],
            edge_out.at[slot, pl.ds(0, 32)],
            edge_out.at[slot, pl.ds(32, 32)],
        )
        return [
            send(whole, edge_side.at[0, slot], right),
            send(whole, edge_side.at[1, slot], left),
            send(lower, edge_corner.at[0, slot], down_right),
            send(lower, edge_corner.at[1, slot], down_left),
            send(upper, edge_corner.at[2, slot], up_right),
            send(upper, edge_corner.at[3, slot], up_left),
        ]

    def chosen(even, even_ok, odd, odd_ok):
        odd_row = lax.broadcasted_iota(jnp.int32, even.shape, 0) % 2 == 1
        even = jnp.where(even_ok, even, 0.0)
        return jnp.where(odd_row, jnp.where(odd_ok, odd, 0.0), even)

    def whole(value, part):
        value = value.astype(f32)
        return jnp.concatenate(
            [value[16 * part : 16 * part + 16], value[16 * part + 32 : 16 * part + 48]], axis=0
        )

    def above(i, slot, part):
        return edge_corner[i, slot].astype(f32)[16 * part + 8 : 16 * part + 16]

    def below(i, slot, part):
        return edge_corner[i, slot].astype(f32)[16 * part : 16 * part + 16]

    def sides(slot):
        return chosen(
            whole(edge_side[0, slot], 0), left_ok, whole(edge_side[1, slot], 0), right_ok
        )

    def upper_edges(slot):
        upper = chosen(above(0, slot, 0), up_ok & left_ok, above(1, slot, 0), up_ok & right_ok)
        return jnp.concatenate([upper, sides(slot)], axis=0)

    def lower_edges(slot):
        return chosen(below(2, slot, 0), down_ok & left_ok, below(3, slot, 0), down_ok & right_ok)

    def outer_edges(slot):
        return jnp.concatenate([upper_edges(slot), lower_edges(slot)], axis=0)

    def inner_edges(slot):
        upper = chosen(above(4, slot, 0), up_ok, above(1, slot, 1), up_ok & right_ok)
        middle = chosen(whole(edge_out[slot], 0), True, whole(edge_side[1, slot], 1), right_ok)
        lower = chosen(below(5, slot, 0), down_ok, below(3, slot, 1), down_ok & right_ok)
        return jnp.concatenate([upper, middle, lower], axis=0)

    def edge_cells(own, past):
        first_half = lax.broadcasted_iota(jnp.int32, (8, 128), 0) < 4
        pieces = []
        for row in range(7):
            mine = pltpu.roll(own[8 * row : 8 * row + 8], 4, 0)
            theirs = 0.0
            if past is not None:
                theirs = pltpu.roll(past[8 * row : 8 * row + 8], 4, 0)
            pieces += [jnp.where(first_half, theirs, mine), jnp.where(first_half, mine, 0.0)]
        pieces.append(jnp.zeros((16, 128), f32))
        return jnp.concatenate(pieces, axis=0)

    def patches(act, t, r):
        return jnp.concatenate(
            [act[t + dt, r : r + 3].reshape(3 * channels, 128) for dt in range(3)], axis=0
        )

    def products(act, weight, cells):
        operand = jnp.concatenate([patches(act, t, r) for t, r in cells], axis=1)
        total = jnp.dot(weight[...], operand, preferred_element_type=f32)
        for i, (t, r) in enumerate(cells):
            sums[t, r] = total[:, 128 * i : 128 * i + 128]

    def stacked(cells):
        moved = [
            (cells if dt == 0 else pltpu.roll(cells, 128 - 2 * dt, 0)).astype(bf16)
            for dt in range(3)
        ]
        rest = jnp.zeros((48, 128), bf16)
        return jnp.concatenate(
            [
                jnp.concatenate([moved[dt][16 * dr : 16 * dr + 80], rest], axis=0)
                for dt in range(3)
                for dr in range(3)
            ],
            axis=1,
        )

    def edge_product(rows, operand):
        return lax.dot_general(
            rows, operand, (((1,), (1,)), ((), ())), preferred_element_type=f32
        )

    def product(rows, operand):
        return jnp.dot(rows, operand, preferred_element_type=f32)

    def edge_products(cells, weight):
        operand = stacked(cells)
        west = edge_product(weight[:channels], operand)
        east = edge_product(weight[2 * channels :], operand)
        edge_sum[...] = jnp.where(
            lane % 2 == 1, pltpu.roll(west, 1, 1), pltpu.roll(east, 127, 1)
        )

    def column_products(outer_cells, inner_cells, weight):
        both = edge_product(weight[...], stacked(outer_cells))
        west, centre, east = (both[i * channels : (i + 1) * channels] for i in range(3))
        edge_sum[...] = jnp.where(
            lane % 2 == 1, pltpu.roll(west, 1, 1), pltpu.roll(east, 127, 1)
        )
        operand = stacked(inner_cells)
        west = edge_product(weight[:channels], operand)
        east = edge_product(weight[2 * channels :], operand)
        column_sum[...] = centre + east + pltpu.roll(west, 1, 1)

    def convolved(t, r):
        k = 16 * r + 2 * t
        ends = pltpu.roll(edge_sum[...], 128 - (k + 1), 1)
        west = jnp.where(lane == 0, ends, pltpu.roll(sums[t, r, :channels], 1, 1))
        east = jnp.where(lane == 127, ends, pltpu.roll(sums[t, r, 2 * channels :], 127, 1))
        return west + sums[t, r, channels : 2 * channels] + east

    def arrange(raw, taps, step, store):
        value = raw.astype(f32)
        for dc in range(3):
            parts = [
                value[:, (3 * tap + dc) * channels : (3 * tap + dc + 1) * channels]
                for tap in range(taps)
            ]
            store(dc, parts)

    def store_conv(i):
        def put(dc, parts):
            rows = slice(dc * channels, (dc + 1) * channels)
            w_conv[i, rows] = jnp.concatenate(parts, axis=1).astype(bf16)
            pad = jnp.zeros((channels, 128 - channels), f32)
            for tap, part in enumerate(parts):
                w_edge[i, rows, tap * 128 : tap * 128 + 128] = jnp.concatenate(
                    [part, pad], axis=1
                ).astype(bf16)

        return put

    def store_down(dc, parts):
        w_down[dc * channels : (dc + 1) * channels] = jnp.concatenate(parts, axis=1).astype(bf16)

    def second(t, rows):
        for r in rows:
            act2[2 + t, 1 + r] = activate(convolved(t, r) + vecs[1], vecs[2], r)

    def third(t):
        for r in range(5):
            residual = x_rows[t, r] if r < 4 else x_low[t]
            total = residual.astype(f32) + (convolved(t, r) + vecs[3])
            ok = inside(r) if r < 4 else low_inside
            block[t, r] = (total * ok).astype(bf16)

    late, early, middle, outer = (2, 3), (0, 1), (1, 2), (0, 3)
    past_frames = pl.ds(0, 2)
    new_frames = pl.ds(4, 2)
    weight1, weight2 = w_conv.at[0], w_conv.at[1]
    edge1, edge2 = w_edge.at[0], w_edge.at[1]

    def take_past_row(act, copy, row):
        arrive(copy)
        for f in (0, 1):
            masked(act, (f, row), group > 0)
        if row == 1:
            return send(act.at[past_frames, 1], act.at[past_frames, 5], up)
        return send(act.at[past_frames, 4], act.at[past_frames, 0], down)

    def take_past_middle(act, copy):
        arrive(copy)
        for f in (0, 1):
            masked(act, (f, slice(2, 4)), group > 0)

    def past_edges(layer, part):
        return jnp.where(group > 0, edge_past[layer, part].astype(f32), 0.0)[:56]

    no_rows = jnp.zeros((8, 128), f32)

    def send_past_edges(layer, parts):
        for i, cells in enumerate(parts):
            edge_on[layer, i] = jnp.concatenate([cells[:40], no_rows], axis=0).astype(bf16)
        some = pl.ds(0, len(parts))
        return send(edge_on.at[layer, some], edge_past.at[layer, some], later)

    def send_past_low(layer, parts):
        for i, cells in enumerate(parts):
            edge_low_on[layer, i] = cells.astype(bf16)
        some = pl.ds(0, len(parts))
        return send(edge_low_on.at[layer, some], edge_low_past.at[layer, some], later)

    def past_edges(layer, part, low=True):
        upper = jnp.where(group > 0, edge_past[layer, part].astype(f32)[:40], 0.0)
        if not low:
            return jnp.concatenate([upper, no_rows, no_rows], axis=0)
        lower = jnp.where(group > 0, edge_low_past[layer, part].astype(f32), 0.0)
        return jnp.concatenate([upper, lower], axis=0)

    spread_vector(0)
    for t in (2, 3, 0, 1):
        first(t)
    fill_picks(pick1, ((0, 127), (1, 0)), ((17, 0),))
    cells = [(t, r) for t in range(4) for r in range(4)]
    gather_edges(
        0, pick1[...], [act1[2 + t, 1 + r] for t, r in cells] + [x_rows[t, r] for t, r in cells]
    )
    pl.semaphore_wait(barrier, sum(there[step].astype(jnp.int32) for step in around))

    outer1 = [send_past_row(act1, 1), send_past_row(act1, 4)]
    edges1 = send_edges(0)
    rows1 = send_rows(act1, 4) + send_rows(act1, 2)
    middle1 = send_past_middle(act1)
    low1 = send(x_rows.at[:, 0], x_low, up)
    w1_load.wait()
    arrange(w_raw[0], 9, 3, store_conv(0))
    for i in range(1, 5):
        spread_vector(i)
    fill_picks(pick2, ((0, 127), (1, 0), (17, 1)))

    for t in late:
        products(act1, weight1, [(t, r) for r in middle])
    arrive(*edges1[:4])
    upper = upper_edges(0)
    edge_own[0, :40] = upper
    past_edges1 = send_past_edges(0, [upper])
    edge_products(edge_cells(jnp.concatenate([upper, no_rows, no_rows], axis=0), None), edge1)
    for t in late:
        second(t, middle)
    middle2 = send_past_middle(act2)
    rims1_low = take_past_row(act1, outer1[0], 1)
    rims1_high = take_past_row(act1, outer1[1], 4)
    wait_upper(act1, 4, rows1[:2])
    wait_upper(act1, 2, rows1[2:])
    products(act1, weight1, [(t, 0) for t in late])
    for t in late:
        second(t, (0,))
    outer2 = [send_past_row(act2, 1)]
    edges2_late = gather_edges2(1, late, 0)
    rows2_late_up = send_rows_up(act2, 4)
    arrive(*edges1[4:])
    low = lower_edges(0)
    edge_own[0, 40:] = low
    past_low1 = send_past_low(0, [low])
    edge_products(edge_cells(edge_own[0], None), edge1)
    wait_lower(act1, 4, rows1[:2])
    wait_lower(act1, 2, rows1[2:])
    products(act1, weight1, [(t, 3) for t in late])
    for t in late:
        second(t, (3,))
    outer2.append(send_past_row(act2, 4))
    edges2_late += gather_edges2(1, late, 1)
    rows2_late = [send_rows_down(act2, 4)] + rows2_late_up

    take_past_middle(act1, middle1)
    for t in early:
        products(act1, weight1, [(t, r) for r in middle])
    arrive(past_edges1)
    edge_products(edge_cells(edge_own[0], past_edges(0, 0, False)), edge1)
    for t in early:
        second(t, middle)
    w2_load.wait()
    arrange(w_raw[1], 9, 3, store_conv(1))
    wait_upper(act1, 0, [rims1_high])
    products(act1, weight1, [(t, 0) for t in early])
    for t in early:
        second(t, (0,))
    edges2_early = gather_edges2(2, early, 0)
    rows2_early_up = send_rows_up(act2, 2)
    arrive(past_low1)
    edge_products(edge_cells(edge_own[0], past_edges(0, 0)), edge1)
    wait_lower(act1, 0, [None, rims1_low])
    products(act1, weight1, [(t, 3) for t in early])
    for t in early:
        second(t, (3,))
    edges2_early += gather_edges2(2, early, 1)
    rows2_early = [send_rows_down(act2, 2)] + rows2_early_up
    arrive(*edges2_late)
    edge_own[0] = outer_edges(1)
    edge_own[1] = inner_edges(1)
    past_edges2 = [
        send_past_edges(1, [edge_own[0], edge_own[1]]),
        send_past_low(1, [edge_own[0, 40:], edge_own[1, 40:]]),
    ]
    for t in late:
        products(act2, weight2, [(t, r) for r in middle])
    take_past_middle(act2, middle2)
    low_row = send(act2.at[past_frames, 2], act2.at[past_frames, 6], up)
    rims2 = [None, take_past_row(act2, outer2[0], 1), low_row]
    rims2[0] = take_past_row(act2, outer2[1], 4)
    for t in early:
        products(act2, weight2, [(t, r) for r in middle])
    wd_load.wait()
    arrange(wd_raw[...], 3, 1, store_down)

    arrive(low1)
    for t in range(4):
        masked(x_low, t, down_ok)
    low_inside = (lane_row < jnp.where(down_ok, col_count, 0)).astype(f32)
    arrive(*edges2_early)
    late_row = lax.broadcasted_iota(jnp.int32, (56, 128), 0) % 8 >= 4
    outer_own = jnp.where(late_row, edge_own[0], outer_edges(2))
    inner_own = jnp.where(late_row, edge_own[1], inner_edges(2))
    arrive(*past_edges2)
    column_products(
        edge_cells(outer_own, past_edges(1, 0)), edge_cells(inner_own, past_edges(1, 1)), edge2
    )
    x_column = [edge_side[1, 0].astype(f32)[16:32], edge_side[1, 0].astype(f32)[48:64]]
    x_column = [x_column[r // 2][8 * (r % 2) : 8 * (r % 2) + 8] for r in range(4)]
    x_column.append(below(3, 0, 1)[:8])
    x_column = sum([[rows, no_rows] for rows in x_column], []) + [jnp.zeros((48, 128), f32)]
    slab_row = lane // 16
    row_inside = ((slab_row < 4) & (slab_row < row_count)) | ((slab_row == 4) & down_ok)
    cells = jnp.concatenate(x_column, axis=0).T[:channels] + (column_sum[...] + vecs[3])
    cells = jnp.where(row_inside & right_ok, cells, 0.0)
    operand = jnp.concatenate(
        [cells, pltpu.roll(cells, 112, 1), pltpu.roll(cells, 96, 1)], axis=0
    ).astype(bf16)
    column_sum[...] = product(w_down[2 * channels :], operand)
    picked = (
        lax.broadcasted_iota(jnp.int32, (256, 128), 0)
        == 2 * lax.broadcasted_iota(jnp.int32, (256, 128), 1)
    ).astype(f32).astype(bf16)
    col_limit = jnp.where(right_ok, 1024, col_count)
    row_limit = jnp.where(down_ok, 1024, row_count)
    stores = []

    def encode(frames):
        for t in frames:
            operand = jnp.concatenate(
                [block[t, 2 * i : 2 * i + 3].reshape(3 * channels, 128) for i in range(2)], axis=1
            )
            total = product(w_down[...], operand)
            for i in range(2):
                sums[t, i] = total[:, 128 * i : 128 * i + 128]
        for t in frames:
            halves = []
            for i in range(2):
                limit = jnp.where(2 * i + 2 <= row_limit, col_limit, 0)
                keep = (lane_row + 2 <= limit).astype(f32)
                ends = pltpu.roll(column_sum[...], 126 - (32 * i + 2 * t + 1), 1)
                total = (
                    sums[t, i, :channels]
                    + pltpu.roll(sums[t, i, channels : 2 * channels], 127, 1)
                    + jnp.where(lane == 126, ends, pltpu.roll(sums[t, i, 2 * channels :], 126, 1))
                )
                halves.append(((total + vecs[4]) * keep).astype(bf16))
            result[t] = product(jnp.concatenate(halves, axis=1), picked).astype(bf16)
            copy = pltpu.make_async_copy(result.at[t], out_hbm.at[t], store_sem.at[t])
            copy.start()
            stores.append(copy)

    for f, copies in ((4, rows2_late), (2, rows2_early)):
        wait_upper(act2, f, copies)
        wait_lower(act2, f, copies)
    for t in late:
        products(act2, weight2, [(t, r) for r in outer])
    wait_low_row(act2, 4, rows2_late)
    wait_low_row(act2, 2, rows2_early)
    products(act2, weight2, [(t, 4) for t in late])
    for t in late:
        third(t)
    encode(late)
    wait_upper(act2, 0, rims2)
    wait_lower(act2, 0, rims2)
    for t in early:
        products(act2, weight2, [(t, r) for r in outer])
    wait_low_row(act2, 0, rims2)
    products(act2, weight2, [(t, 4) for t in early])
    for t in early:
        third(t)
    encode(early)
    for copy, ok in sends:
        pl.when(ok)(copy.wait_send)
    for copy in stores:
        copy.wait()


def per_device(grid_rows, groups, video, links, extents, g1, w1, b1, g2, w2, b2, wd, bd):
    _, frames, channels, slab_rows, slab_cols = video.shape
    x = video.reshape(frames, channels * slab_rows, slab_cols)
    vectors = [v.reshape(1, channels) for v in (g1, b1, g2, b2, bd)]
    g1, b1, g2, b2, bd = vectors
    vmem = pltpu.VMEM
    out = pl.pallas_call(
        functools.partial(kernel, GRID_COLUMN_COUNT, grid_rows, groups),
        out_shape=jax.ShapeDtypeStruct((frames, channels, 128), bf16),
        in_specs=[pl.BlockSpec(memory_space=pl.ANY)] * 11,
        out_specs=pl.BlockSpec(memory_space=pl.ANY),
        scratch_shapes=[
            pltpu.SMEM((1, 4), jnp.int32),
            pltpu.SMEM((1, 2), jnp.int32),
            vmem((4, channels * 4, 128), bf16),
            vmem((channels * 4, 128), f32),
            vmem((4, 4, channels, 128), bf16),
            vmem((2, channels, 27 * channels), bf16),
            vmem((channels, 9 * channels), bf16),
            vmem((5, 1, channels), f32),
            vmem((5, channels, 128), f32),
            vmem((2, 3 * channels, 9 * channels), bf16),
            vmem((2, 3 * channels, 9 * 128), bf16),
            vmem((3 * channels, 3 * channels), bf16),
            vmem((4, channels, 128), bf16),
            vmem((6, 6, channels, 128), bf16),
            vmem((6, 7, channels, 128), bf16),
            vmem((4, 5, channels, 128), bf16),
            vmem((4, 5, 3 * channels, 128), f32),
            vmem((channels, 128), f32),
            vmem((channels, 128), f32),
            vmem((64, 32 * 128), bf16),
            vmem((64, 16 * 128), bf16),
            vmem((2, 56, 128), f32),
            vmem((3, 64, 128), bf16),
            vmem((2, 3, 64, 128), bf16),
            vmem((6, 3, 32, 128), bf16),
            vmem((2, 2, 48, 128), bf16),
            vmem((2, 2, 48, 128), bf16),
            vmem((2, 2, 16, 128), bf16),
            vmem((2, 2, 16, 128), bf16),
            vmem((4, channels, 128), bf16),
            pltpu.SemaphoreType.DMA((14,)),
            pltpu.SemaphoreType.DMA((COPIES,)),
            pltpu.SemaphoreType.DMA((COPIES,)),
            pltpu.SemaphoreType.DMA((4,)),
        ],
        compiler_params=pltpu.CompilerParams(
            collective_id=0, has_side_effects=True, vmem_limit_bytes=60 * 2**20
        ),
    )(links, extents, x, g1, w1, b1, g2, w2, b2, wd, bd)
    return out[None]


def solution(mesh):
    placed = (P("tile", "tm", None, None, None), P("tile", None), P("tile", None)) + (P(),) * 8
    return jax.shard_map(
        functools.partial(
            per_device, mesh.shape["tile"] // GRID_COLUMN_COUNT, mesh.shape["tm"]
        ),
        mesh=mesh,
        in_specs=placed,
        out_specs=P("tile", "tm", None, None),
        check_vma=False,
    )
```

```python
import functools

import jax
import jax.numpy as jnp
from jax import lax
from jax.experimental import pallas as pl
from jax.experimental.pallas import tpu as pltpu
from jax.sharding import PartitionSpec as P

GRID_COLUMN_COUNT = 8
MESH = pl.DeviceIdType.MESH
norm_eps = 1e-06
f32 = jnp.float32
bf16 = jnp.bfloat16

COPIES = 64


def kernel(
    grid_cols,
    grid_rows,
    groups,
    links_hbm,
    extents_hbm,
    x_hbm,
    g1_hbm,
    w1_hbm,
    b1_hbm,
    g2_hbm,
    w2_hbm,
    b2_hbm,
    wd_hbm,
    bd_hbm,
    out_hbm,
    links,
    extents,
    x_raw,
    spread,
    x_rows,
    w_raw,
    wd_raw,
    vec_raw,
    vecs,
    w_conv,
    w_edge,
    w_down,
    x_low,
    act1,
    act2,
    block,
    sums,
    edge_sum,
    column_sum,
    pick1,
    pick2,
    edge_own,
    edge_out,
    edge_side,
    edge_corner,
    edge_on,
    edge_past,
    edge_low_on,
    edge_low_past,
    result,
    load_sem,
    send_sem,
    recv_sem,
    store_sem,
):
    channels = vecs.shape[1]
    tile = lax.axis_index("tile")
    group = lax.axis_index("tm")
    grow, gcol = tile // grid_cols, tile % grid_cols
    up, down, left, right = (-1, 0, 0), (1, 0, 0), (0, -1, 0), (0, 1, 0)
    up_left, up_right, down_left, down_right = (-1, -1, 0), (-1, 1, 0), (1, -1, 0), (1, 1, 0)
    later, before = (0, 0, 1), (0, 0, -1)
    around = (up, down, left, right, up_left, up_right, down_left, down_right, later, before)

    def device_at(step):
        row = (grow + step[0] + grid_rows) % grid_rows
        col = (gcol + step[1] + grid_cols) % grid_cols
        return (row * grid_cols + col, (group + step[2] + groups) % groups)

    def is_there(step):
        there = None
        for at, move, size in zip((grow, gcol, group), step, (grid_rows, grid_cols, groups)):
            if move:
                ok = at + move >= 0 if move < 0 else at + move < size
                there = ok if there is None else there & ok
        return there

    there = {step: is_there(step) for step in around}

    barrier = pltpu.get_barrier_semaphore()
    for step in around:

        @pl.when(there[step])
        def _(step=step):
            pl.semaphore_signal(
                barrier, inc=1, device_id=device_at(step), device_id_type=MESH
            )

    loads = []

    def load(src, dst):
        copy = pltpu.make_async_copy(src, dst, load_sem.at[len(loads)])
        copy.start()
        loads.append(copy)
        return copy

    x_loads = {t: load(x_hbm.at[t], x_raw.at[t]) for t in (2, 3, 0, 1)}
    vec_loads = [
        load(ref, vec_raw.at[i]) for i, ref in enumerate((g1_hbm, b1_hbm, g2_hbm, b2_hbm, bd_hbm))
    ]
    scalar_loads = [load(links_hbm, links), load(extents_hbm, extents)]
    w1_load = load(w1_hbm, w_raw.at[0])
    w2_load = load(w2_hbm, w_raw.at[1])
    wd_load = load(wd_hbm, wd_raw)

    sends = []

    def send(src, dst, step):
        i = len(sends)
        copy = pltpu.make_async_remote_copy(
            src_ref=src,
            dst_ref=dst,
            send_sem=send_sem.at[i],
            recv_sem=recv_sem.at[i],
            device_id=device_at(step),
            device_id_type=MESH,
        )
        pl.when(there[step])(copy.start)
        sends.append((copy, there[step]))
        return copy, there[tuple(-move for move in step)]

    def arrive(*copies):
        for copy, ok in copies:
            pl.when(ok)(copy.wait_recv)

    lane = lax.broadcasted_iota(jnp.int32, (channels, 128), 1)
    lane_row = lax.broadcasted_iota(jnp.int32, (1, 128), 1)
    for copy in scalar_loads:
        copy.wait()
    up_ok, down_ok = links[0, 0] >= 0, links[0, 1] >= 0
    left_ok, right_ok = links[0, 2] >= 0, links[0, 3] >= 0
    row_count, col_count = extents[0, 0], extents[0, 1]

    def inside(r):
        cols = jnp.where(r < row_count, col_count, 0)
        return (lane_row < cols).astype(f32)

    def activate(values, gain, r):
        mean_square = jnp.mean(values * values, axis=0, keepdims=True)
        normed = values * lax.rsqrt(mean_square + norm_eps) * gain
        return (normed / (1.0 + jnp.exp(-normed)) * inside(r)).astype(bf16)

    diagonal = lax.broadcasted_iota(jnp.int32, (channels, channels), 0) == lax.broadcasted_iota(
        jnp.int32, (channels, channels), 1
    )

    def spread_vector(i):
        vec_loads[i].wait()
        column = jnp.sum(jnp.where(diagonal, vec_raw[i], 0.0), axis=1, keepdims=True)
        vecs[i] = jnp.broadcast_to(column, (channels, 128))

    def first(t):
        x_loads[t].wait()
        spread[...] = x_raw[t].astype(f32)
        gain = vecs[0]
        for r in range(4):
            values = spread[pl.ds(r, channels, stride=4), :]
            x_rows[t, r] = values.astype(bf16)
            act1[2 + t, 1 + r] = activate(values, gain, r)

    def masked(ref, index, ok):
        ref[index] = jnp.where(ok, ref[index], jnp.zeros_like(ref[index]))

    def send_rows_up(act, f):
        frames = pl.ds(f, 2)
        copies = [send(act.at[frames, 1], act.at[frames, 5], up)]
        if act.shape[1] > 6:
            copies.append(send(act.at[frames, 2], act.at[frames, 6], up))
        return copies

    def send_rows_down(act, f):
        frames = pl.ds(f, 2)
        return send(act.at[frames, 4], act.at[frames, 0], down)

    def send_rows(act, f):
        return [send_rows_down(act, f)] + send_rows_up(act, f)

    def wait_upper(act, f, copies):
        arrive(copies[0])
        for g in (f, f + 1):
            masked(act, (g, 0), up_ok)

    def wait_lower(act, f, copies):
        arrive(copies[1])
        for g in (f, f + 1):
            masked(act, (g, 5), down_ok)

    def wait_low_row(act, f, copies):
        arrive(copies[2])
        for g in (f, f + 1):
            masked(act, (g, 6), down_ok)

    def send_past_row(act, row):
        return send(act.at[new_frames, row], act.at[past_frames, row], later)

    def send_past_middle(act):
        return send(act.at[new_frames, pl.ds(2, 2)], act.at[past_frames, pl.ds(2, 2)], later)

    pick_row = lax.broadcasted_iota(jnp.int32, (64, 128), 0)
    pick_lane = lax.broadcasted_iota(jnp.int32, (64, 128), 1)

    def picks(*pairs):
        hit = False
        for row, col in pairs:
            hit = hit | ((pick_row == row) & (pick_lane == col))
        return jnp.where(hit, 1.0, 0.0).astype(bf16)

    def edge_row(t, r):
        return r // 2 * 32 + r % 2 * 8 + t * 2

    def fill_picks(ref, *wanted):
        for i, pairs in enumerate(wanted):
            for t in range(4):
                for r in range(4):
                    at = ((i * 4 + t) * 4 + r) * 128
                    ref[:, at : at + 128] = picks(
                        *[(edge_row(t, r) + row, col) for row, col in pairs]
                    )

    def gather_edges(slot, pick, cells):
        rows = lax.dot_general(
            pick,
            jnp.concatenate(cells, axis=1),
            (((1,), (1,)), ((), ())),
            preferred_element_type=f32,
        )
        edge_out[slot, :, :channels] = rows.astype(bf16)
        edge_out[slot, :, channels:] = jnp.zeros((64, 128 - channels), bf16)

    def gather_edges2(slot, frames, half):
        mine = pl.ds(32 * half, 32)
        cells = [act2[2 + t, 1 + r] for t in frames for r in (2 * half, 2 * half + 1)]
        pick = jnp.concatenate(
            [pick2[mine, t * 512 + half * 256 : t * 512 + half * 256 + 256] for t in frames],
            axis=1,
        )
        rows = lax.dot_general(
            pick,
            jnp.concatenate(cells, axis=1),
            (((1,), (1,)), ((), ())),
            preferred_element_type=f32,
        )
        edge_out[slot, mine, :channels] = rows.astype(bf16)
        edge_out[slot, mine, channels:] = jnp.zeros((32, 128 - channels), bf16)
        part = edge_out.at[slot, mine]
        first, steps = (
            (2, (up_right, up_left, up)) if half == 0 else (0, (down_right, down_left, down))
        )
        slots = (first, first + 1, 5 if half == 0 else 4)
        return [
            send(part, edge_side.at[0, slot, mine], right),
            send(part, edge_side.at[1, slot, mine], left),
        ] + [send(part, edge_corner.at[i, slot], step) for i, step in zip(slots, steps)]

    def send_edges(slot):
        whole, upper, lower = (
            edge_out.at[slot],
            edge_out.at[slot, pl.ds(0, 32)],
            edge_out.at[slot, pl.ds(32, 32)],
        )
        return [
            send(whole, edge_side.at[0, slot], right),
            send(whole, edge_side.at[1, slot], left),
            send(lower, edge_corner.at[0, slot], down_right),
            send(lower, edge_corner.at[1, slot], down_left),
            send(upper, edge_corner.at[2, slot], up_right),
            send(upper, edge_corner.at[3, slot], up_left),
        ]

    def chosen(even, even_ok, odd, odd_ok):
        odd_row = lax.broadcasted_iota(jnp.int32, even.shape, 0) % 2 == 1
        even = jnp.where(even_ok, even, 0.0)
        return jnp.where(odd_row, jnp.where(odd_ok, odd, 0.0), even)

    def whole(value, part):
        value = value.astype(f32)
        return jnp.concatenate(
            [value[16 * part : 16 * part + 16], value[16 * part + 32 : 16 * part + 48]], axis=0
        )

    def above(i, slot, part):
        return edge_corner[i, slot].astype(f32)[16 * part + 8 : 16 * part + 16]

    def below(i, slot, part):
        return edge_corner[i, slot].astype(f32)[16 * part : 16 * part + 16]

    def sides(slot):
        return chosen(
            whole(edge_side[0, slot], 0), left_ok, whole(edge_side[1, slot], 0), right_ok
        )

    def upper_edges(slot):
        upper = chosen(above(0, slot, 0), up_ok & left_ok, above(1, slot, 0), up_ok & right_ok)
        return jnp.concatenate([upper, sides(slot)], axis=0)

    def lower_edges(slot):
        return chosen(below(2, slot, 0), down_ok & left_ok, below(3, slot, 0), down_ok & right_ok)

    def outer_edges(slot):
        return jnp.concatenate([upper_edges(slot), lower_edges(slot)], axis=0)

    def inner_edges(slot):
        upper = chosen(above(4, slot, 0), up_ok, above(1, slot, 1), up_ok & right_ok)
        middle = chosen(whole(edge_out[slot], 0), True, whole(edge_side[1, slot], 1), right_ok)
        lower = chosen(below(5, slot, 0), down_ok, below(3, slot, 1), down_ok & right_ok)
        return jnp.concatenate([upper, middle, lower], axis=0)

    def edge_cells(own, past):
        first_half = lax.broadcasted_iota(jnp.int32, (8, 128), 0) < 4
        pieces = []
        for row in range(7):
            mine = pltpu.roll(own[8 * row : 8 * row + 8], 4, 0)
            theirs = 0.0
            if past is not None:
                theirs = pltpu.roll(past[8 * row : 8 * row + 8], 4, 0)
            pieces += [jnp.where(first_half, theirs, mine), jnp.where(first_half, mine, 0.0)]
        pieces.append(jnp.zeros((16, 128), f32))
        return jnp.concatenate(pieces, axis=0)

    def patches(act, t, r):
        return jnp.concatenate(
            [act[t + dt, r : r + 3].reshape(3 * channels, 128) for dt in range(3)], axis=0
        )

    def products(act, weight, cells):
        operand = jnp.concatenate([patches(act, t, r) for t, r in cells], axis=1)
        total = jnp.dot(weight[...], operand, preferred_element_type=f32)
        for i, (t, r) in enumerate(cells):
            sums[t, r] = total[:, 128 * i : 128 * i + 128]

    def stacked(cells):
        moved = [
            (cells if dt == 0 else pltpu.roll(cells, 128 - 2 * dt, 0)).astype(bf16)
            for dt in range(3)
        ]
        rest = jnp.zeros((48, 128), bf16)
        return jnp.concatenate(
            [
                jnp.concatenate([moved[dt][16 * dr : 16 * dr + 80], rest], axis=0)
                for dt in range(3)
                for dr in range(3)
            ],
            axis=1,
        )

    def edge_product(rows, operand):
        return lax.dot_general(
            rows, operand, (((1,), (1,)), ((), ())), preferred_element_type=f32
        )

    def product(rows, operand):
        return jnp.dot(rows, operand, preferred_element_type=f32)

    def edge_products(cells, weight):
        operand = stacked(cells)
        west = edge_product(weight[:channels], operand)
        east = edge_product(weight[2 * channels :], operand)
        edge_sum[...] = jnp.where(
            lane % 2 == 1, pltpu.roll(west, 1, 1), pltpu.roll(east, 127, 1)
        )

    def column_products(outer_cells, inner_cells, weight):
        both = edge_product(weight[...], stacked(outer_cells))
        west, centre, east = (both[i * channels : (i + 1) * channels] for i in range(3))
        edge_sum[...] = jnp.where(
            lane % 2 == 1, pltpu.roll(west, 1, 1), pltpu.roll(east, 127, 1)
        )
        operand = stacked(inner_cells)
        west = edge_product(weight[:channels], operand)
        east = edge_product(weight[2 * channels :], operand)
        column_sum[...] = centre + east + pltpu.roll(west, 1, 1)

    def convolved(t, r):
        k = 16 * r + 2 * t
        ends = pltpu.roll(edge_sum[...], 128 - (k + 1), 1)
        west = jnp.where(lane == 0, ends, pltpu.roll(sums[t, r, :channels], 1, 1))
        east = jnp.where(lane == 127, ends, pltpu.roll(sums[t, r, 2 * channels :], 127, 1))
        return west + sums[t, r, channels : 2 * channels] + east

    def arrange(raw, taps, step, store):
        value = raw.astype(f32)
        for dc in range(3):
            parts = [
                value[:, (3 * tap + dc) * channels : (3 * tap + dc + 1) * channels]
                for tap in range(taps)
            ]
            store(dc, parts)

    def store_conv(i):
        def put(dc, parts):
            rows = slice(dc * channels, (dc + 1) * channels)
            w_conv[i, rows] = jnp.concatenate(parts, axis=1).astype(bf16)
            pad = jnp.zeros((channels, 128 - channels), f32)
            for tap, part in enumerate(parts):
                w_edge[i, rows, tap * 128 : tap * 128 + 128] = jnp.concatenate(
                    [part, pad], axis=1
                ).astype(bf16)

        return put

    def store_down(dc, parts):
        w_down[dc * channels : (dc + 1) * channels] = jnp.concatenate(parts, axis=1).astype(bf16)

    def second(t, rows):
        for r in rows:
            act2[2 + t, 1 + r] = activate(convolved(t, r) + vecs[1], vecs[2], r)

    def third(t):
        for r in range(5):
            residual = x_rows[t, r] if r < 4 else x_low[t]
            total = residual.astype(f32) + (convolved(t, r) + vecs[3])
            ok = inside(r) if r < 4 else low_inside
            block[t, r] = (total * ok).astype(bf16)

    late, early, middle, outer = (2, 3), (0, 1), (1, 2), (0, 3)
    past_frames = pl.ds(0, 2)
    new_frames = pl.ds(4, 2)
    weight1, weight2 = w_conv.at[0], w_conv.at[1]
    edge1, edge2 = w_edge.at[0], w_edge.at[1]

    def take_past_row(act, copy, row):
        arrive(copy)
        for f in (0, 1):
            masked(act, (f, row), group > 0)
        if row == 1:
            return send(act.at[past_frames, 1], act.at[past_frames, 5], up)
        return send(act.at[past_frames, 4], act.at[past_frames, 0], down)

    def take_past_middle(act, copy):
        arrive(copy)
        for f in (0, 1):
            masked(act, (f, slice(2, 4)), group > 0)

    def past_edges(layer, part):
        return jnp.where(group > 0, edge_past[layer, part].astype(f32), 0.0)[:56]

    no_rows = jnp.zeros((8, 128), f32)

    def send_past_edges(layer, parts):
        for i, cells in enumerate(parts):
            edge_on[layer, i] = jnp.concatenate([cells[:40], no_rows], axis=0).astype(bf16)
        some = pl.ds(0, len(parts))
        return send(edge_on.at[layer, some], edge_past.at[layer, some], later)

    def send_past_low(layer, parts):
        for i, cells in enumerate(parts):
            edge_low_on[layer, i] = cells.astype(bf16)
        some = pl.ds(0, len(parts))
        return send(edge_low_on.at[layer, some], edge_low_past.at[layer, some], later)

    def past_edges(layer, part, low=True):
        upper = jnp.where(group > 0, edge_past[layer, part].astype(f32)[:40], 0.0)
        if not low:
            return jnp.concatenate([upper, no_rows, no_rows], axis=0)
        lower = jnp.where(group > 0, edge_low_past[layer, part].astype(f32), 0.0)
        return jnp.concatenate([upper, lower], axis=0)

    spread_vector(0)
    for t in (2, 3, 0, 1):
        first(t)
    fill_picks(pick1, ((0, 127), (1, 0)), ((17, 0),))
    cells = [(t, r) for t in range(4) for r in range(4)]
    gather_edges(
        0, pick1[...], [act1[2 + t, 1 + r] for t, r in cells] + [x_rows[t, r] for t, r in cells]
    )
    pl.semaphore_wait(barrier, sum(there[step].astype(jnp.int32) for step in around))

    edges1 = send_edges(0)
    outer1 = [send_past_row(act1, 1), send_past_row(act1, 4)]
    rows1 = send_rows(act1, 4) + send_rows(act1, 2)
    middle1 = send_past_middle(act1)
    low1 = send(x_rows.at[:, 0], x_low, up)
    w1_load.wait()
    arrange(w_raw[0], 9, 3, store_conv(0))
    for i in range(1, 5):
        spread_vector(i)
    fill_picks(pick2, ((0, 127), (1, 0), (17, 1)))

    for t in late:
        products(act1, weight1, [(t, r) for r in middle])
    arrive(*edges1[:4])
    upper = upper_edges(0)
    edge_own[0, :40] = upper
    past_edges1 = send_past_edges(0, [upper])
    edge_products(edge_cells(jnp.concatenate([upper, no_rows, no_rows], axis=0), None), edge1)
    for t in late:
        second(t, middle)
    middle2 = send_past_middle(act2)
    rims1_low = take_past_row(act1, outer1[0], 1)
    rims1_high = take_past_row(act1, outer1[1], 4)
    wait_upper(act1, 4, rows1[:2])
    wait_upper(act1, 2, rows1[2:])
    products(act1, weight1, [(t, 0) for t in late])
    for t in late:
        second(t, (0,))
    outer2 = [send_past_row(act2, 1)]
    edges2_late = gather_edges2(1, late, 0)
    rows2_late_up = send_rows_up(act2, 4)
    arrive(*edges1[4:])
    low = lower_edges(0)
    edge_own[0, 40:] = low
    past_low1 = send_past_low(0, [low])
    edge_products(edge_cells(edge_own[0], None), edge1)
    wait_lower(act1, 4, rows1[:2])
    wait_lower(act1, 2, rows1[2:])
    products(act1, weight1, [(t, 3) for t in late])
    for t in late:
        second(t, (3,))
    outer2.append(send_past_row(act2, 4))
    edges2_late += gather_edges2(1, late, 1)
    rows2_late = [send_rows_down(act2, 4)] + rows2_late_up

    take_past_middle(act1, middle1)
    for t in early:
        products(act1, weight1, [(t, r) for r in middle])
    arrive(past_edges1)
    edge_products(edge_cells(edge_own[0], past_edges(0, 0, False)), edge1)
    for t in early:
        second(t, middle)
    w2_load.wait()
    arrange(w_raw[1], 9, 3, store_conv(1))
    wait_upper(act1, 0, [rims1_high])
    products(act1, weight1, [(t, 0) for t in early])
    for t in early:
        second(t, (0,))
    edges2_early = gather_edges2(2, early, 0)
    rows2_early_up = send_rows_up(act2, 2)
    arrive(past_low1)
    edge_products(edge_cells(edge_own[0], past_edges(0, 0)), edge1)
    wait_lower(act1, 0, [None, rims1_low])
    products(act1, weight1, [(t, 3) for t in early])
    for t in early:
        second(t, (3,))
    edges2_early += gather_edges2(2, early, 1)
    rows2_early = [send_rows_down(act2, 2)] + rows2_early_up
    rims2 = [None, take_past_row(act2, outer2[0], 1), None]
    take_past_middle(act2, middle2)
    rims2[2] = send(act2.at[past_frames, 2], act2.at[past_frames, 6], up)
    rims2[0] = take_past_row(act2, outer2[1], 4)
    arrive(*edges2_late)
    edge_own[0] = outer_edges(1)
    edge_own[1] = inner_edges(1)
    past_edges2 = [
        send_past_edges(1, [edge_own[0], edge_own[1]]),
        send_past_low(1, [edge_own[0, 40:], edge_own[1, 40:]]),
    ]
    for t in late:
        products(act2, weight2, [(t, r) for r in middle])
    for t in early:
        products(act2, weight2, [(t, r) for r in middle])
    wd_load.wait()
    arrange(wd_raw[...], 3, 1, store_down)

    arrive(low1)
    for t in range(4):
        masked(x_low, t, down_ok)
    low_inside = (lane_row < jnp.where(down_ok, col_count, 0)).astype(f32)
    arrive(*edges2_early)
    late_row = lax.broadcasted_iota(jnp.int32, (56, 128), 0) % 8 >= 4
    outer_own = jnp.where(late_row, edge_own[0], outer_edges(2))
    inner_own = jnp.where(late_row, edge_own[1], inner_edges(2))
    arrive(*past_edges2)
    column_products(
        edge_cells(outer_own, past_edges(1, 0)), edge_cells(inner_own, past_edges(1, 1)), edge2
    )
    x_column = [edge_side[1, 0].astype(f32)[16:32], edge_side[1, 0].astype(f32)[48:64]]
    x_column = [x_column[r // 2][8 * (r % 2) : 8 * (r % 2) + 8] for r in range(4)]
    x_column.append(below(3, 0, 1)[:8])
    x_column = sum([[rows, no_rows] for rows in x_column], []) + [jnp.zeros((48, 128), f32)]
    slab_row = lane // 16
    row_inside = ((slab_row < 4) & (slab_row < row_count)) | ((slab_row == 4) & down_ok)
    cells = jnp.concatenate(x_column, axis=0).T[:channels] + (column_sum[...] + vecs[3])
    cells = jnp.where(row_inside & right_ok, cells, 0.0)
    operand = jnp.concatenate(
        [cells, pltpu.roll(cells, 112, 1), pltpu.roll(cells, 96, 1)], axis=0
    ).astype(bf16)
    column_sum[...] = product(w_down[2 * channels :], operand)
    picked = (
        lax.broadcasted_iota(jnp.int32, (256, 128), 0)
        == 2 * lax.broadcasted_iota(jnp.int32, (256, 128), 1)
    ).astype(f32).astype(bf16)
    col_limit = jnp.where(right_ok, 1024, col_count)
    row_limit = jnp.where(down_ok, 1024, row_count)
    stores = []

    def encode(frames):
        for t in frames:
            operand = jnp.concatenate(
                [block[t, 2 * i : 2 * i + 3].reshape(3 * channels, 128) for i in range(2)], axis=1
            )
            total = product(w_down[...], operand)
            for i in range(2):
                sums[t, i] = total[:, 128 * i : 128 * i + 128]
        for t in frames:
            halves = []
            for i in range(2):
                limit = jnp.where(2 * i + 2 <= row_limit, col_limit, 0)
                keep = (lane_row + 2 <= limit).astype(f32)
                ends = pltpu.roll(column_sum[...], 126 - (32 * i + 2 * t + 1), 1)
                total = (
                    sums[t, i, :channels]
                    + pltpu.roll(sums[t, i, channels : 2 * channels], 127, 1)
                    + jnp.where(lane == 126, ends, pltpu.roll(sums[t, i, 2 * channels :], 126, 1))
                )
                halves.append(((total + vecs[4]) * keep).astype(bf16))
            result[t] = product(jnp.concatenate(halves, axis=1), picked).astype(bf16)
            copy = pltpu.make_async_copy(result.at[t], out_hbm.at[t], store_sem.at[t])
            copy.start()
            stores.append(copy)

    for f, copies in ((4, rows2_late), (2, rows2_early)):
        wait_upper(act2, f, copies)
        wait_lower(act2, f, copies)
    for t in late:
        products(act2, weight2, [(t, r) for r in outer])
    wait_low_row(act2, 4, rows2_late)
    wait_low_row(act2, 2, rows2_early)
    products(act2, weight2, [(t, 4) for t in late])
    for t in late:
        third(t)
    encode(late)
    wait_upper(act2, 0, rims2)
    wait_lower(act2, 0, rims2)
    for t in early:
        products(act2, weight2, [(t, r) for r in outer])
    wait_low_row(act2, 0, rims2)
    products(act2, weight2, [(t, 4) for t in early])
    for t in early:
        third(t)
    encode(early)
    for copy, ok in sends:
        pl.when(ok)(copy.wait_send)
    for copy in stores:
        copy.wait()


def per_device(grid_rows, groups, video, links, extents, g1, w1, b1, g2, w2, b2, wd, bd):
    _, frames, channels, slab_rows, slab_cols = video.shape
    x = video.reshape(frames, channels * slab_rows, slab_cols)
    vectors = [v.reshape(1, channels) for v in (g1, b1, g2, b2, bd)]
    g1, b1, g2, b2, bd = vectors
    vmem = pltpu.VMEM
    out = pl.pallas_call(
        functools.partial(kernel, GRID_COLUMN_COUNT, grid_rows, groups),
        out_shape=jax.ShapeDtypeStruct((frames, channels, 128), bf16),
        in_specs=[pl.BlockSpec(memory_space=pl.ANY)] * 11,
        out_specs=pl.BlockSpec(memory_space=pl.ANY),
        scratch_shapes=[
            pltpu.SMEM((1, 4), jnp.int32),
            pltpu.SMEM((1, 2), jnp.int32),
            vmem((4, channels * 4, 128), bf16),
            vmem((channels * 4, 128), f32),
            vmem((4, 4, channels, 128), bf16),
            vmem((2, channels, 27 * channels), bf16),
            vmem((channels, 9 * channels), bf16),
            vmem((5, 1, channels), f32),
            vmem((5, channels, 128), f32),
            vmem((2, 3 * channels, 9 * channels), bf16),
            vmem((2, 3 * channels, 9 * 128), bf16),
            vmem((3 * channels, 3 * channels), bf16),
            vmem((4, channels, 128), bf16),
            vmem((6, 6, channels, 128), bf16),
            vmem((6, 7, channels, 128), bf16),
            vmem((4, 5, channels, 128), bf16),
            vmem((4, 5, 3 * channels, 128), f32),
            vmem((channels, 128), f32),
            vmem((channels, 128), f32),
            vmem((64, 32 * 128), bf16),
            vmem((64, 16 * 128), bf16),
            vmem((2, 56, 128), f32),
            vmem((3, 64, 128), bf16),
            vmem((2, 3, 64, 128), bf16),
            vmem((6, 3, 32, 128), bf16),
            vmem((2, 2, 48, 128), bf16),
            vmem((2, 2, 48, 128), bf16),
            vmem((2, 2, 16, 128), bf16),
            vmem((2, 2, 16, 128), bf16),
            vmem((4, channels, 128), bf16),
            pltpu.SemaphoreType.DMA((14,)),
            pltpu.SemaphoreType.DMA((COPIES,)),
            pltpu.SemaphoreType.DMA((COPIES,)),
            pltpu.SemaphoreType.DMA((4,)),
        ],
        compiler_params=pltpu.CompilerParams(
            collective_id=0, has_side_effects=True, vmem_limit_bytes=60 * 2**20
        ),
    )(links, extents, x, g1, w1, b1, g2, w2, b2, wd, bd)
    return out[None]


def solution(mesh):
    placed = (P("tile", "tm", None, None, None), P("tile", None), P("tile", None)) + (P(),) * 8
    return jax.shard_map(
        functools.partial(
            per_device, mesh.shape["tile"] // GRID_COLUMN_COUNT, mesh.shape["tm"]
        ),
        mesh=mesh,
        in_specs=placed,
        out_specs=P("tile", "tm", None, None),
        check_vma=False,
    )
```
